256 devices in a mesh: row: 32 (over y_lo, z, core), col: 8 (over x, y_hi).
Axes of the slice: x: 4, y: 4 (y_hi: 2, y_lo: 2; y = y_hi * 2 + y_lo), z: 8, core: 2. Of those that a mesh axis runs over, the one named last changes fastest.
Arguments:
- pair_input: bfloat16 [512, 512, 128], P('row', 'col'), may hold values from -6 to 6
- norm_gain: float32 [128], replicated, may hold values from 0.1 to 1.9
- norm_bias: float32 [128], replicated, may hold values from -3 to 3
- weights: bfloat16 [4, 128, 128], replicated, may hold values from -0.5 to 0.5
- cotangent: bfloat16 [512, 512, 128], P('row', 'col'), may hold values from -0.29882812 to 0.29882812
Outputs:
- pair_grad: bfloat16 [512, 512, 128], P('row', 'col')
- weight_grad: float32 [4, 128, 128], replicated
- gain_grad: float32 [128], replicated
- bias_grad: float32 [128], replicated
The draws below stay inside these ranges and needn't reach their ends.
All inputs are finite; a program needn't handle non-finite values.
Results may differ from the reference program's by a relative error of at most 0.0068.
Values may be sent and summed in bfloat16 or wider, within the bound.
A program may use at most 192 MiB of HBM per device.

```python
import jax
import jax.numpy as jnp
from jax import lax

C = 128
H = 128
N = 512


def shard_levels(own_key, extent, pieces, low, top_value):
    def one(dim, blocks):
        steps = jax.random.uniform(jax.random.fold_in(jax.random.fold_in(own_key, 6), dim), (blocks,), jnp.float32, low / len(pieces), top_value / len(pieces))
        return jnp.repeat(jnp.exp(steps), extent[dim] // blocks).reshape((-1,) + (1,) * (len(extent) - dim - 1))

    gain = one(*pieces[0])
    for cut in pieces[1:]:
        gain = gain * one(*cut)
    return gain


def bell_draw(rng, extent, deviation, most, shards=(), dtype=jnp.bfloat16):
    entries = deviation * jax.random.normal(rng, extent, jnp.float32)
    if shards:
        entries = entries * shard_levels(rng, extent, shards, -0.22, 0.18)
    return jnp.clip(entries, -most, most).astype(dtype)


def setup_inputs(seed: int = 0) -> dict:
    seeds = jax.random.split(jax.random.key(seed), 6)
    pair_input = bell_draw(seeds[0], (N, N, C), 1.0, 6.0, ((0, 32), (1, 8)))
    norm_gain = jnp.clip(1.0 + 0.18 * jax.random.normal(seeds[1], (C,), jnp.float32), 0.1, 1.9)
    norm_bias = bell_draw(seeds[2], (C,), 0.5, 3.0, (), jnp.float32)
    weights = bell_draw(seeds[3], (4, C, H), C ** -0.5, 0.5)
    cotangent = bell_draw(seeds[4], (N, N, H), 0.05, 0.29882812, ((0, 32), (1, 8)))
    return {"pair_input": pair_input, "norm_gain": norm_gain, "norm_bias": norm_bias, "weights": weights, "cotangent": cotangent}


def reference(pair_input, norm_gain, norm_bias, weights, cotangent):
    values = pair_input.astype(jnp.float32)
    average = lax.optimization_barrier(jnp.mean(values, -1, keepdims=True))
    centred = values - average
    inverse = jax.lax.rsqrt(lax.optimization_barrier(jnp.mean(centred * centred, -1, keepdims=True)) + 1e-05)
    scaled = centred * inverse
    normed = (scaled * norm_gain + norm_bias).astype(jnp.bfloat16)
    weights32 = weights.astype(jnp.float32)
    preact = jnp.einsum('ijc,mch->ijmh', normed.astype(jnp.float32), weights32)
    sigmoid_first = jax.nn.sigmoid(preact[:, :, 0])
    sigmoid_second = jax.nn.sigmoid(preact[:, :, 2])
    first = (sigmoid_first * preact[:, :, 1]).astype(jnp.bfloat16)
    second = (sigmoid_second * preact[:, :, 3]).astype(jnp.bfloat16)
    cot32 = cotangent.astype(jnp.float32)
    grad_first = jnp.einsum('ijh,jkh->ikh', cot32, second.astype(jnp.float32))
    grad_second = jnp.einsum('ijh,ikh->jkh', cot32, first.astype(jnp.float32))
    preact_grad = jnp.stack([grad_first * preact[:, :, 1] * sigmoid_first * (1.0 - sigmoid_first), grad_first * sigmoid_first, grad_second * preact[:, :, 3] * sigmoid_second * (1.0 - sigmoid_second), grad_second * sigmoid_second], 2).astype(jnp.bfloat16)
    preact_wide = preact_grad.astype(jnp.float32)
    normed_grad = jnp.einsum('ijmh,mch->ijc', preact_wide, weights32)
    factor = 1.0 / N
    weight_grad = jnp.einsum('ijc,ijmh->mch', normed.astype(jnp.float32), preact_wide) * factor
    gain_grad = lax.optimization_barrier(jnp.sum(scaled * normed_grad, (0, 1))) * factor
    bias_grad = lax.optimization_barrier(jnp.sum(normed_grad, (0, 1))) * factor
    scaled_grad = normed_grad * norm_gain
    pair_grad = inverse * (scaled_grad - lax.optimization_barrier(jnp.mean(scaled_grad, -1, keepdims=True)) - scaled * lax.optimization_barrier(jnp.mean(scaled_grad * scaled, -1, keepdims=True)))
    return (pair_grad.astype(jnp.bfloat16), weight_grad, gain_grad, bias_grad)
```

```python
import jax
import jax.numpy as jnp
from jax import lax
from jax.experimental import pallas as pl
from jax.experimental.pallas import tpu as pltpu
from jax.sharding import PartitionSpec as P

MESH = pl.DeviceIdType.MESH
F32 = jnp.float32
BF16 = jnp.bfloat16

ROWS, COLS, DEPTH, XS = 32, 8, 8, 4
R, W, H, N = 16, 64, 128, 512
PAIRS = R * W
OWN = H // ROWS // 2
PLANES = H // 2

COT, OPS, SECOND, FIRST, PART, DEEP, WHOLE, SMALL_Z, SMALL_COL, SMALL_ROW, RING = range(11)


def nt(a, b):
    return lax.dot_general(a, b, (((1,), (1,)), ((), ())), preferred_element_type=F32)


def tn(a, b):
    return lax.dot_general(a, b, (((0,), (0,)), ((), ())), preferred_element_type=F32)


def kernel(
    pair_ref, gain_ref, bias_ref, w_ref, cot_ref,
    out_ref, wg_ref, gg_ref, bg_ref,
    stage, send_cot, send_ops, cots, ops, blocks, acc, out_first, out_second, got_first, got_second,
    factors, scaled, normed, inverse, w_t, w_cat, grads, w_part, parts, deeps, wholes, small_z, small_col, small_row,
    send_sem, recv_sem, ring_sem, local_sem,
):
    row, col = lax.axis_index("row"), lax.axis_index("col")
    z, core, y_lo = lax.rem(row // 2, DEPTH), lax.rem(row, 2), row // (2 * DEPTH)
    x, y_hi = col // 2, lax.rem(col, 2)
    left_lanes = lax.broadcasted_iota(jnp.int32, (W, 2 * W), 1) < W
    eye = (
        lax.broadcasted_iota(jnp.int32, (H, H), 0) == lax.broadcasted_iota(jnp.int32, (H, H), 1)
    ).astype(F32).astype(BF16)

    def plane_row(s):
        return (s // 2) * (2 * DEPTH) + z * 2 + lax.rem(s, 2)

    def send(src, dst, kind, device, arrived=None):
        pltpu.make_async_remote_copy(
            src_ref=src,
            dst_ref=dst,
            send_sem=send_sem.at[kind],
            recv_sem=recv_sem.at[kind] if arrived is None else arrived,
            device_id=device,
            device_id_type=MESH,
        ).start()

    def wait(ref, sem):
        pltpu.make_async_copy(ref, ref, sem).wait()

    def rows_of(p):
        return pl.ds(pl.multiple_of(p * R, R), R)

    def planes_of(p):
        return pl.ds(p * OWN, OWN)

    def spread(t, value):
        low, high = value[:PLANES], value[PLANES:]
        stage[pl.ds(2 * t * PLANES, PLANES), :] = jnp.where(left_lanes, low, pltpu.roll(high, W, 1))
        stage[pl.ds((2 * t + 1) * PLANES, PLANES), :] = jnp.where(left_lanes, pltpu.roll(low, W, 1), high)

    barrier = pltpu.get_barrier_semaphore()

    @pl.loop(1, ROWS)
    def _(d):
        pl.semaphore_signal(barrier, inc=1, device_id=(lax.rem(row + d, ROWS), col), device_id_type=MESH)

    @pl.loop(0, 4 * (COLS - 1))
    def _(d):
        pl.semaphore_signal(
            barrier,
            inc=1,
            device_id=(plane_row(d // (COLS - 1)), lax.rem(col + 1 + lax.rem(d, COLS - 1), COLS)),
            device_id_type=MESH,
        )

    for t in range(R // 2):
        spread(t, nt(eye, cot_ref[t * 2 * W : (t + 1) * 2 * W, :]))

    @pl.loop(0, PLANES, unroll=8)
    def _(h):
        send_cot[h] = stage[pl.ds(h, R, stride=PLANES), :].astype(BF16)

    pl.semaphore_wait(barrier, ROWS - 1 + 4 * (COLS - 1))

    @pl.loop(1, ROWS)
    def _(d):
        p = lax.rem(row + d, ROWS)
        send(send_cot.at[planes_of(p)], cots.at[col, :, rows_of(row), :], COT, (p, col))

    own_cot = pltpu.make_async_copy(send_cot.at[planes_of(row)], cots.at[col, :, rows_of(row), :], local_sem.at[COT])
    own_cot.start()

    gain = jnp.transpose(jnp.broadcast_to(gain_ref[...], (H, H)))
    bias = jnp.transpose(jnp.broadcast_to(bias_ref[...], (H, H)))
    for m in range(4):
        w_t[m * H : (m + 1) * H, :] = jnp.transpose(w_ref[m].astype(F32)).astype(BF16)
        w_cat[:, m * H : (m + 1) * H] = w_ref[m]
    for t in range(R // 2):
        lanes = slice(t * 2 * W, (t + 1) * 2 * W)
        values = nt(eye, pair_ref[lanes, :])
        centred = values - jnp.mean(values, 0, keepdims=True)
        inv = lax.rsqrt(jnp.mean(centred * centred, 0, keepdims=True) + 1e-05)
        scale = centred * inv
        inverse[t : t + 1, :] = inv
        scaled[:, lanes] = scale
        normed[:, lanes] = (scale * gain + bias).astype(BF16)
    for side in range(2):
        for t in range(R // 2):
            lanes = slice(t * 2 * W, (t + 1) * 2 * W)
            pre = jnp.dot(w_t[2 * side * H : 2 * (side + 1) * H, :], normed[:, lanes], preferred_element_type=F32)
            gate, value = jax.nn.sigmoid(pre[:H]), pre[H:]
            product = gate * value
            factors[2 * side * H : (2 * side + 1) * H, lanes] = product * (1.0 - gate)
            factors[(2 * side + 1) * H : 2 * (side + 1) * H, lanes] = gate
            spread(t, product)

        @pl.loop(0, ROWS, unroll=4)
        def _(p):
            for k in range(OWN):
                send_ops[p, side * OWN + k] = stage[pl.ds(p * OWN + k, R, stride=PLANES), :].astype(BF16)

    @pl.loop(1, ROWS)
    def _(d):
        p = lax.rem(row + d, ROWS)
        send(send_ops.at[p], ops.at[:, rows_of(row), :], OPS, (p, col))

    own_ops = pltpu.make_async_copy(send_ops.at[row], ops.at[:, rows_of(row), :], local_sem.at[OPS])
    own_ops.start()

    own_cot.wait()
    wait(cots.at[0, :, : N - R, :], recv_sem.at[COT])
    mate = col + 1 - 2 * y_hi
    right_x, left_x, far_x = lax.rem(x + 1, XS), lax.rem(x + XS - 1, XS), lax.rem(x + 2, XS)
    right, left = right_x * 2 + y_hi, left_x * 2 + y_hi

    def pass_on(q, k, to):
        send(cots.at[q, k], cots.at[q, k], RING, (row, to), ring_sem.at[q, k])

    def arrived(q, k):
        wait(cots.at[q, k], ring_sem.at[q, k])

    pass_on(col, 0, right)
    pass_on(col, 1, left)
    pass_on(col, 0, mate)
    pass_on(col, 1, mate)
    pass_on(col, 1, right)
    pass_on(col, 0, left)
    arrived(mate, 0)
    pass_on(mate, 0, right)
    pass_on(mate, 0, left)
    arrived(mate, 1)
    pass_on(mate, 1, left)
    pass_on(mate, 1, right)
    arrived(left, 0)
    pass_on(left, 0, right)
    arrived(right, 1)
    pass_on(right, 1, left)

    own_ops.wait()
    wait(ops.at[:, : N - R, :], recv_sem.at[OPS])
    for k in range(OWN):
        for q in range(COLS):
            block = ops[OWN + k, q * W : (q + 1) * W, :].astype(F32)
            blocks[k, q * 2 * W : q * 2 * W + W, :] = jnp.where(left_lanes, block, 0.0).astype(BF16)
            blocks[k, q * 2 * W + W : (q + 1) * 2 * W, :] = jnp.where(left_lanes, 0.0, block).astype(BF16)

    def products(at, opening):
        for k in range(OWN):
            cot = jnp.concatenate([cots[2 * at, k], cots[2 * at + 1, k]], 1)
            term = jnp.dot(
                cot, blocks[k, pl.ds(pl.multiple_of(at * 4 * W, 4 * W), 4 * W), :], preferred_element_type=F32
            )
            if opening:
                acc[k] = term
            else:
                acc[k] += term
            both = tn(cot, ops[k])
            for y in range(2):
                out_second[k, pl.ds(pl.multiple_of((2 * at + y) * W, W), W), :] = jnp.where(
                    left_lanes, both[2 * y * W : (2 * y + 1) * W], both[(2 * y + 1) * W : 2 * (y + 1) * W]
                ).astype(BF16)

        @pl.loop(0, ROWS // XS)
        def _(d):
            p = at * (ROWS // XS) + d

            @pl.when(p != row)
            def _():
                send(out_second.at[:, rows_of(p), :], got_second.at[planes_of(row)], SECOND, (p, col))

            @pl.when(p == row)
            def _():
                copy = pltpu.make_async_copy(
                    out_second.at[:, rows_of(p), :], got_second.at[planes_of(row)], local_sem.at[SECOND]
                )
                copy.start()
                copy.wait()

    products(x, True)
    mate_left, mate_right = left_x * 2 + 1 - y_hi, right_x * 2 + 1 - y_hi
    arrived(mate_left, 0)
    pass_on(mate_left, 0, right)
    arrived(mate_right, 1)
    pass_on(mate_right, 1, left)
    arrived(left, 1)
    arrived(mate_left, 1)
    products(left_x, False)
    arrived(right, 0)
    arrived(mate_right, 0)
    products(right_x, False)
    for k in range(2):
        arrived(far_x * 2, k)
        arrived(far_x * 2 + 1, k)
    products(far_x, False)

    for k in range(OWN):
        out_first[k] = acc[k].astype(BF16)

    @pl.loop(1, ROWS)
    def _(d):
        p = lax.rem(row + d, ROWS)
        send(out_first.at[:, rows_of(p), :], got_first.at[planes_of(row)], FIRST, (p, col))

    own_first = pltpu.make_async_copy(
        out_first.at[:, rows_of(row), :], got_first.at[planes_of(row)], local_sem.at[FIRST]
    )
    own_first.start()

    def gather_in(side, got):
        @pl.loop(0, PLANES, unroll=8)
        def _(h):
            stage[pl.ds(pl.multiple_of(h * R, R), R), :] = got[h].astype(F32)

        for t in range(R // 2):
            lanes = slice(t * 2 * W, (t + 1) * 2 * W)
            even = stage[pl.ds(2 * t, PLANES, stride=R), :]
            odd = stage[pl.ds(2 * t + 1, PLANES, stride=R), :]
            grad = jnp.concatenate(
                [
                    jnp.where(left_lanes, even, pltpu.roll(odd, W, 1)),
                    jnp.where(left_lanes, pltpu.roll(even, W, 1), odd),
                ],
                0,
            )
            for m in (2 * side, 2 * side + 1):
                grads[m * H : (m + 1) * H, lanes] = (grad * factors[m * H : (m + 1) * H, lanes]).astype(BF16)

    def weight_part(side):
        part = nt(normed[...], grads[2 * side * H : 2 * (side + 1) * H, :])
        for m in range(2):
            w_part[(2 * side + m) * H : (2 * side + m + 1) * H, :] = part[:, m * H : (m + 1) * H]

    wait(got_second.at[: PLANES - OWN], recv_sem.at[SECOND])
    gather_in(1, got_second)
    weight_part(1)
    own_first.wait()
    wait(got_first.at[: PLANES - OWN], recv_sem.at[FIRST])
    gather_in(0, got_first)
    weight_part(0)

    spot = (y_lo * 2 + core) * COLS + col

    def of_plane(d):
        g = lax.rem(spot + d, 4 * COLS)
        return g, (plane_row(g // COLS), lax.rem(g, COLS))

    @pl.loop(1, 4 * COLS)
    def _(d):
        g, device = of_plane(d)
        send(w_part.at[rows_of(g), :], parts.at[spot], PART, device)

    parts[spot] = w_part[rows_of(spot), :]

    gain_sum = jnp.zeros((H, 2 * W), F32)
    bias_sum = jnp.zeros((H, 2 * W), F32)
    for t in range(R // 2):
        lanes = slice(t * 2 * W, (t + 1) * 2 * W)
        grad = jnp.dot(w_cat[...], grads[:, lanes], preferred_element_type=F32)
        scale = scaled[:, lanes]
        gain_sum += grad * scale
        bias_sum += grad
        grad = grad * gain
        pair = inverse[t : t + 1, :] * (
            grad - jnp.mean(grad, 0, keepdims=True) - scale * jnp.mean(grad * scale, 0, keepdims=True)
        )
        out_ref[lanes, :] = jnp.transpose(pair).astype(BF16)
    gain_sum = jnp.sum(jnp.transpose(gain_sum), 0, keepdims=True)
    bias_sum = jnp.sum(jnp.transpose(bias_sum), 0, keepdims=True)
    small_z[z] = jnp.concatenate([gain_sum, bias_sum, jnp.zeros((6, H), F32)], 0)

    def z_peer(d):
        return (y_lo * 2 * DEPTH + lax.rem(z + d, DEPTH) * 2 + core, col)

    @pl.loop(1, DEPTH)
    def _(d):
        send(small_z.at[z], small_z.at[z], SMALL_Z, z_peer(d))

    wait(parts.at[: 4 * COLS - 1], recv_sem.at[PART])
    deeps[z] = jnp.sum(parts[...], 0)

    @pl.loop(1, DEPTH)
    def _(d):
        send(deeps.at[z], deeps.at[z], DEEP, z_peer(d))

    wait(small_z.at[: DEPTH - 1], recv_sem.at[SMALL_Z])
    small_col[col] = jnp.sum(small_z[...], 0)

    @pl.loop(1, COLS)
    def _(d):
        send(small_col.at[col], small_col.at[col], SMALL_COL, (row, lax.rem(col + d, COLS)))

    wait(deeps.at[: DEPTH - 1], recv_sem.at[DEEP])
    wholes[spot] = jnp.sum(deeps[...], 0) * (1.0 / N)

    @pl.loop(1, 4 * COLS)
    def _(d):
        _, device = of_plane(d)
        send(wholes.at[spot], wholes.at[spot], WHOLE, device)

    wait(small_col.at[: COLS - 1], recv_sem.at[SMALL_COL])
    quarter = y_lo * 2 + core
    small_row[quarter] = jnp.sum(small_col[...], 0)

    @pl.loop(1, 4)
    def _(d):
        send(small_row.at[quarter], small_row.at[quarter], SMALL_ROW, (plane_row(lax.rem(quarter + d, 4)), col))

    wait(small_row.at[:3], recv_sem.at[SMALL_ROW])
    total = jnp.sum(small_row[...], 0) * (1.0 / N)
    gg_ref[...] = total[0:1]
    bg_ref[...] = total[1:2]

    wait(wholes.at[: 4 * COLS - 1], recv_sem.at[WHOLE])
    wg_ref[...] = wholes[...].reshape(4 * H, H)

    wait(cots.at[0, :, : N - R, :], send_sem.at[COT])
    wait(ops.at[:, : N - R, :], send_sem.at[OPS])
    wait(cots.at[: COLS - 1], send_sem.at[RING])
    wait(got_second.at[: PLANES - OWN], send_sem.at[SECOND])
    wait(got_first.at[: PLANES - OWN], send_sem.at[FIRST])
    wait(parts.at[: 4 * COLS - 1], send_sem.at[PART])
    wait(deeps.at[: DEPTH - 1], send_sem.at[DEEP])
    wait(wholes.at[: 4 * COLS - 1], send_sem.at[WHOLE])
    wait(small_z.at[: DEPTH - 1], send_sem.at[SMALL_Z])
    wait(small_col.at[: COLS - 1], send_sem.at[SMALL_COL])
    wait(small_row.at[:3], send_sem.at[SMALL_ROW])


def local(pair_input, norm_gain, norm_bias, weights, cotangent):
    vmem = pl.BlockSpec(memory_space=pltpu.VMEM)
    out, weight_grad, gain_grad, bias_grad = pl.pallas_call(
        kernel,
        out_shape=(
            jax.ShapeDtypeStruct((PAIRS, H), BF16),
            jax.ShapeDtypeStruct((4 * H, H), F32),
            jax.ShapeDtypeStruct((1, H), F32),
            jax.ShapeDtypeStruct((1, H), F32),
        ),
        in_specs=[vmem] * 5,
        out_specs=(vmem,) * 4,
        scratch_shapes=[
            pltpu.VMEM((PAIRS, 2 * W), F32),
            pltpu.VMEM((PLANES, R, 2 * W), BF16),
            pltpu.VMEM((ROWS, 2 * OWN, R, 2 * W), BF16),
            pltpu.VMEM((COLS, OWN, N, 2 * W), BF16),
            pltpu.VMEM((2 * OWN, N, 2 * W), BF16),
            pltpu.VMEM((OWN, 2 * N, 2 * W), BF16),
            pltpu.VMEM((OWN, N, 2 * W), F32),
            pltpu.VMEM((OWN, N, 2 * W), BF16),
            pltpu.VMEM((OWN, N, 2 * W), BF16),
            pltpu.VMEM((PLANES, R, 2 * W), BF16),
            pltpu.VMEM((PLANES, R, 2 * W), BF16),
            pltpu.VMEM((4 * H, PAIRS), F32),
            pltpu.VMEM((H, PAIRS), F32),
            pltpu.VMEM((H, PAIRS), BF16),
            pltpu.VMEM((R // 2, 2 * W), F32),
            pltpu.VMEM((4 * H, H), BF16),
            pltpu.VMEM((H, 4 * H), BF16),
            pltpu.VMEM((4 * H, PAIRS), BF16),
            pltpu.VMEM((4 * H, H), F32),
            pltpu.VMEM((4 * COLS, R, H), F32),
            pltpu.VMEM((DEPTH, R, H), F32),
            pltpu.VMEM((4 * COLS, R, H), F32),
            pltpu.VMEM((DEPTH, 8, H), F32),
            pltpu.VMEM((COLS, 8, H), F32),
            pltpu.VMEM((4, 8, H), F32),
            pltpu.SemaphoreType.DMA((11,)),
            pltpu.SemaphoreType.DMA((11,)),
            pltpu.SemaphoreType.DMA((COLS, OWN)),
            pltpu.SemaphoreType.DMA((4,)),
        ],
        compiler_params=pltpu.CompilerParams(
            collective_id=0, has_side_effects=True, vmem_limit_bytes=40 * 1024 * 1024
        ),
        name="triangle_backward",
    )(
        pair_input.reshape(PAIRS, H),
        norm_gain.reshape(1, H),
        norm_bias.reshape(1, H),
        weights,
        cotangent.reshape(PAIRS, H),
    )
    return (
        out.reshape(R, W, H),
        weight_grad.reshape(4, H, H),
        gain_grad.reshape(H),
        bias_grad.reshape(H),
    )


def solution(mesh):
    placed = (P("row", "col", None), P(), P(), P(), P("row", "col", None))
    return jax.shard_map(
        local,
        mesh=mesh,
        in_specs=placed,
        out_specs=(P("row", "col", None), P(), P(), P()),
        check_vma=False,
    )
```

```python
import jax
import jax.numpy as jnp
from jax import lax
from jax.experimental import pallas as pl
from jax.experimental.pallas import tpu as pltpu
from jax.sharding import PartitionSpec as P

MESH = pl.DeviceIdType.MESH
F32 = jnp.float32
BF16 = jnp.bfloat16

ROWS, COLS, DEPTH, XS, YS = 32, 8, 8, 4, 2
R, W, H, N = 16, 64, 128, 512
PAIRS = R * W
BAND = ROWS * YS
SPOTS = COLS * 4
PART = 4 * H // SPOTS // 2

COT, OP_FIRST, OP_SECOND, FIRST, SECOND, PART_FIRST, PART_SECOND, DEEP, WHOLE, SMALL_Z, SMALL_COL, SMALL_ROW, RING = range(13)


def nt(a, b):
    return lax.dot_general(a, b, (((1,), (1,)), ((), ())), preferred_element_type=F32)


def tn(a, b):
    return lax.dot_general(a, b, (((0,), (0,)), ((), ())), preferred_element_type=F32)


def kernel(
    pair_hbm, gain_hbm, bias_hbm, w_hbm, cot_hbm,
    out_ref, wg_ref, gg_ref, bg_ref,
    pair_ref, gain_ref, bias_ref, w_ref, cot_ref,
    stage, send_cot, send_first, send_second, cots, firsts, seconds, blocks, out_first, out_second, got_first, got_second,
    factors, scaled, normed, inverse, w_t, w_cat, grads, normed_grad, w_part, parts, deeps, wholes, small_z, small_col, small_row,
    send_sem, recv_sem, ring_sem, local_sem, load_sem,
):
    row, col = lax.axis_index("row"), lax.axis_index("col")
    z, core, y_lo = lax.rem(row // 2, DEPTH), lax.rem(row, 2), row // (2 * DEPTH)
    x, y_hi = col // YS, lax.rem(col, YS)
    y = y_hi * 2 + y_lo
    plane = y_hi * ROWS + row

    loads = [
        pltpu.make_async_copy(src, dst, load_sem.at[i])
        for i, (src, dst) in enumerate(
            ((cot_hbm, cot_ref), (pair_hbm, pair_ref), (w_hbm, w_ref), (gain_hbm, gain_ref), (bias_hbm, bias_ref))
        )
    ]
    for load in loads:
        load.start()

    left_lanes = lax.broadcasted_iota(jnp.int32, (W, 2 * W), 1) < W
    eye = (
        lax.broadcasted_iota(jnp.int32, (H, H), 0) == lax.broadcasted_iota(jnp.int32, (H, H), 1)
    ).astype(F32).astype(BF16)

    def plane_row(s):
        return (s // 2) * (2 * DEPTH) + z * 2 + lax.rem(s, 2)

    def send(src, dst, kind, device, arrived=None):
        pltpu.make_async_remote_copy(
            src_ref=src,
            dst_ref=dst,
            send_sem=send_sem.at[kind],
            recv_sem=recv_sem.at[kind] if arrived is None else arrived,
            device_id=device,
            device_id_type=MESH,
        ).start()

    def wait(ref, sem):
        pltpu.make_async_copy(ref, ref, sem).wait()

    def rows_of(p):
        return pl.ds(pl.multiple_of(p * R, R), R)

    near = []
    for dy in (2, 1, 3, 0):
        other_y = lax.rem(y + dy, 4)
        for dc in (1, 0):
            near.append((other_y // 2, lax.rem(other_y, 2) * (2 * DEPTH) + lax.rem(core + dc, 2)))

    def each_of_band(act):
        @pl.loop(0, DEPTH - 1)
        def _(s):
            dz = DEPTH // 2 + ((s + 1) // 2) * (1 - 2 * lax.rem(s, 2))
            base = lax.rem(z + dz, DEPTH) * 2
            for there, offset in near:
                act(there, base + offset)

        for there, offset in near[:-1]:
            act(there, z * 2 + offset)

    barrier = pltpu.get_barrier_semaphore()
    right_x, left_x, far_x = lax.rem(x + 1, XS), lax.rem(x + XS - 1, XS), lax.rem(x + 2, XS)
    right, left = right_x * YS + y_hi, left_x * YS + y_hi

    def greet(there, p):
        pl.semaphore_signal(barrier, inc=1, device_id=(p, x * YS + there), device_id_type=MESH)

    each_of_band(greet)
    for to in (right, left):
        pl.semaphore_signal(barrier, inc=1, device_id=(row, to), device_id_type=MESH)

    def spread(t, value):
        low, high = value[:BAND], value[BAND:]
        stage[pl.ds(2 * t * BAND, BAND), :] = jnp.where(left_lanes, low, pltpu.roll(high, W, 1))
        stage[pl.ds((2 * t + 1) * BAND, BAND), :] = jnp.where(left_lanes, pltpu.roll(low, W, 1), high)

    def to_planes(planes):
        @pl.loop(0, BAND, unroll=8)
        def _(h):
            planes[h] = stage[pl.ds(h, R, stride=BAND), :].astype(BF16)

    def scatter(planes, dst, kind):
        def act(there, p):
            send(planes.at[there * ROWS + p], dst, kind, (p, x * YS + there))

        each_of_band(act)
        own = pltpu.make_async_copy(planes.at[plane], dst, local_sem.at[kind])
        own.start()
        return own

    loads[0].wait()
    for t in range(R // 2):
        spread(t, nt(eye, cot_ref[t * 2 * W : (t + 1) * 2 * W, :]))
    to_planes(send_cot)
    pl.semaphore_wait(barrier, BAND - 1 + 2)
    own_cot = scatter(send_cot, cots.at[x, y_hi, rows_of(row), :], COT)

    for load in loads[1:]:
        load.wait()
    gain = jnp.transpose(jnp.broadcast_to(gain_ref[...], (H, H)))
    bias = jnp.transpose(jnp.broadcast_to(bias_ref[...], (H, H)))
    for m in range(4):
        w_t[m * H : (m + 1) * H, :] = jnp.transpose(w_ref[m].astype(F32)).astype(BF16)
        w_cat[:, m * H : (m + 1) * H] = w_ref[m]
    for t in range(R // 2):
        lanes = slice(t * 2 * W, (t + 1) * 2 * W)
        values = nt(eye, pair_ref[lanes, :])
        centred = values - jnp.mean(values, 0, keepdims=True)
        inv = lax.rsqrt(jnp.mean(centred * centred, 0, keepdims=True) + 1e-05)
        scale = centred * inv
        inverse[t : t + 1, :] = inv
        scaled[:, lanes] = scale
        normed[:, lanes] = (scale * gain + bias).astype(BF16)

    def gated(side, planes):
        for t in range(R // 2):
            lanes = slice(t * 2 * W, (t + 1) * 2 * W)
            pre = jnp.dot(w_t[2 * side * H : 2 * (side + 1) * H, :], normed[:, lanes], preferred_element_type=F32)
            gate, value = jax.nn.sigmoid(pre[:H]), pre[H:]
            product = gate * value
            factors[2 * side * H : (2 * side + 1) * H, lanes] = product * (1.0 - gate)
            factors[(2 * side + 1) * H : 2 * (side + 1) * H, lanes] = gate
            spread(t, product)
        to_planes(planes)

    gated(0, send_first)
    own_op_first = scatter(send_first, firsts.at[y_hi, rows_of(row), :], OP_FIRST)
    gated(1, send_second)

    def pass_on(at, k, to):
        send(cots.at[at, k], cots.at[at, k], RING, (row, to), ring_sem.at[at, k])

    def arrived(at, k):
        wait(cots.at[at, k], ring_sem.at[at, k])

    own_cot.wait()
    wait(send_cot.at[: BAND - 1], recv_sem.at[COT])
    pass_on(x, 0, right)
    pass_on(x, 1, left)
    pass_on(x, 1, right)
    pass_on(x, 0, left)
    own_op_second = scatter(send_second, seconds.at[y_hi, rows_of(row), :], OP_SECOND)
    arrived(left_x, 0)
    pass_on(left_x, 0, right)
    arrived(right_x, 1)
    pass_on(right_x, 1, left)

    own_op_first.wait()
    wait(send_first.at[: BAND - 1], recv_sem.at[OP_FIRST])

    def second_products(at):
        cot = jnp.concatenate([cots[at, 0], cots[at, 1]], 1)
        both = tn(cot, jnp.concatenate([firsts[0], firsts[1]], 1))
        for there in range(YS):
            lanes = slice(there * 2 * W, (there + 1) * 2 * W)
            for k in range(YS):
                out_second[there, pl.ds(pl.multiple_of((YS * at + k) * W, W), W), :] = jnp.where(
                    left_lanes, both[2 * k * W : (2 * k + 1) * W, lanes], both[(2 * k + 1) * W : 2 * (k + 1) * W, lanes]
                ).astype(BF16)

        @pl.loop(0, ROWS // XS)
        def _(d):
            p = at * (ROWS // XS) + d
            mate = 1 - y_hi
            send(out_second.at[mate, rows_of(p), :], got_second.at[plane], SECOND, (p, x * YS + mate))

            @pl.when(p != row)
            def _():
                send(out_second.at[y_hi, rows_of(p), :], got_second.at[plane], SECOND, (p, col))

            @pl.when(p == row)
            def _():
                copy = pltpu.make_async_copy(
                    out_second.at[y_hi, rows_of(p), :], got_second.at[plane], local_sem.at[SECOND]
                )
                copy.start()
                copy.wait()

    second_products(x)
    arrived(right_x, 0)
    second_products(right_x)
    arrived(left_x, 1)
    second_products(left_x)
    arrived(far_x, 0)
    arrived(far_x, 1)
    second_products(far_x)

    own_op_second.wait()
    wait(send_second.at[: BAND - 1], recv_sem.at[OP_SECOND])
    for q in range(COLS):
        for there in range(YS):
            block = seconds[there, q * W : (q + 1) * W, :].astype(F32)
            lanes = slice(there * 2 * W, (there + 1) * 2 * W)
            blocks[q * 2 * W : q * 2 * W + W, lanes] = jnp.where(left_lanes, block, 0.0).astype(BF16)
            blocks[q * 2 * W + W : (q + 1) * 2 * W, lanes] = jnp.where(left_lanes, 0.0, block).astype(BF16)
    for half in range(2):
        rows = slice(half * N // 2, (half + 1) * N // 2)
        cot = jnp.concatenate([cots[q // YS, q % YS, rows] for q in range(COLS)], 1)
        term = jnp.dot(cot, blocks[...], preferred_element_type=F32)
        for there in range(YS):
            out_first[there, rows, :] = term[:, there * 2 * W : (there + 1) * 2 * W].astype(BF16)

    def return_first(there, p):
        send(out_first.at[there, rows_of(p), :], got_first.at[plane], FIRST, (p, x * YS + there))

    each_of_band(return_first)
    own_first = pltpu.make_async_copy(out_first.at[y_hi, rows_of(row), :], got_first.at[plane], local_sem.at[FIRST])
    own_first.start()

    def gather_in(side, got):
        @pl.loop(0, BAND, unroll=8)
        def _(h):
            stage[pl.ds(pl.multiple_of(h * R, R), R), :] = got[h].astype(F32)

        for t in range(R // 2):
            lanes = slice(t * 2 * W, (t + 1) * 2 * W)
            even = stage[pl.ds(2 * t, BAND, stride=R), :]
            odd = stage[pl.ds(2 * t + 1, BAND, stride=R), :]
            grad = jnp.concatenate(
                [
                    jnp.where(left_lanes, even, pltpu.roll(odd, W, 1)),
                    jnp.where(left_lanes, pltpu.roll(even, W, 1), odd),
                ],
                0,
            )
            for m in (2 * side, 2 * side + 1):
                grads[m * H : (m + 1) * H, lanes] = (grad * factors[m * H : (m + 1) * H, lanes]).astype(BF16)

    spot = (y_lo * 2 + core) * COLS + col

    def each_spot(act):
        @pl.loop(1, SPOTS)
        def _(d):
            g = lax.rem(spot + d, SPOTS)
            act(g, (plane_row(g // COLS), lax.rem(g, COLS)))

    def weight_part(side, kind):
        part = nt(normed[...], grads[2 * side * H : 2 * (side + 1) * H, :])
        for m in range(2):
            w_part[(2 * side + m) * H : (2 * side + m + 1) * H, :] = part[:, m * H : (m + 1) * H]

        def share(g):
            return pl.ds(pl.multiple_of(2 * side * H + g * PART, PART), PART)

        mine = slice(side * PART, (side + 1) * PART)
        each_spot(lambda g, device: send(w_part.at[share(g), :], parts.at[spot, mine, :], kind, device))
        parts[spot, mine, :] = w_part[share(spot), :]

    wait(send_cot.at[: BAND - 1], recv_sem.at[SECOND])
    gather_in(1, got_second)
    weight_part(1, PART_SECOND)
    own_first.wait()
    wait(send_cot.at[: BAND - 1], recv_sem.at[FIRST])
    gather_in(0, got_first)
    weight_part(0, PART_FIRST)

    gain_sum = jnp.zeros((H, 2 * W), F32)
    bias_sum = jnp.zeros((H, 2 * W), F32)
    for t in range(R // 2):
        lanes = slice(t * 2 * W, (t + 1) * 2 * W)
        grad = jnp.dot(w_cat[...], grads[:, lanes], preferred_element_type=F32)
        normed_grad[:, lanes] = grad
        gain_sum += grad * scaled[:, lanes]
        bias_sum += grad
    gain_sum = jnp.sum(jnp.transpose(gain_sum), 0, keepdims=True)
    bias_sum = jnp.sum(jnp.transpose(bias_sum), 0, keepdims=True)
    small_z[z] = jnp.concatenate([gain_sum, bias_sum, jnp.zeros((6, H), F32)], 0)

    def z_peer(d):
        return (y_lo * 2 * DEPTH + lax.rem(z + d, DEPTH) * 2 + core, col)

    @pl.loop(1, DEPTH)
    def _(d):
        send(small_z.at[z], small_z.at[z], SMALL_Z, z_peer(d))

    wait(parts.at[: SPOTS - 1, :PART, :], recv_sem.at[PART_SECOND])
    wait(parts.at[: SPOTS - 1, :PART, :], recv_sem.at[PART_FIRST])
    deeps[z] = jnp.sum(parts[...], 0)

    @pl.loop(1, DEPTH)
    def _(d):
        send(deeps.at[z], deeps.at[z], DEEP, z_peer(d))

    for t in range(R // 2):
        lanes = slice(t * 2 * W, (t + 1) * 2 * W)
        scale = scaled[:, lanes]
        grad = normed_grad[:, lanes] * gain
        pair = inverse[t : t + 1, :] * (
            grad - jnp.mean(grad, 0, keepdims=True) - scale * jnp.mean(grad * scale, 0, keepdims=True)
        )
        out_ref[lanes, :] = jnp.transpose(pair).astype(BF16)

    wait(small_z.at[: DEPTH - 1], recv_sem.at[SMALL_Z])
    small_col[col] = jnp.sum(small_z[...], 0)

    @pl.loop(1, COLS)
    def _(d):
        send(small_col.at[col], small_col.at[col], SMALL_COL, (row, lax.rem(col + d, COLS)))

    wait(deeps.at[: DEPTH - 1], recv_sem.at[DEEP])
    wholes[spot] = jnp.sum(deeps[...], 0) * (1.0 / N)
    each_spot(lambda g, device: send(wholes.at[spot], wholes.at[spot], WHOLE, device))

    wait(small_col.at[: COLS - 1], recv_sem.at[SMALL_COL])
    quarter = y_lo * 2 + core
    small_row[quarter] = jnp.sum(small_col[...], 0)

    @pl.loop(1, 4)
    def _(d):
        send(small_row.at[quarter], small_row.at[quarter], SMALL_ROW, (plane_row(lax.rem(quarter + d, 4)), col))

    for kind in (COT, OP_FIRST, OP_SECOND, FIRST, SECOND):
        wait(send_cot.at[: BAND - 1], send_sem.at[kind])
    wait(cots.at[: XS - 1], send_sem.at[RING])
    wait(parts.at[: SPOTS - 1, :PART, :], send_sem.at[PART_SECOND])
    wait(parts.at[: SPOTS - 1, :PART, :], send_sem.at[PART_FIRST])
    wait(deeps.at[: DEPTH - 1], send_sem.at[DEEP])
    wait(small_z.at[: DEPTH - 1], send_sem.at[SMALL_Z])
    wait(small_col.at[: COLS - 1], send_sem.at[SMALL_COL])

    wait(wholes.at[: SPOTS - 1], recv_sem.at[WHOLE])
    for side in range(2):
        wg_ref[2 * side * H : 2 * (side + 1) * H, :] = wholes[:, side * PART : (side + 1) * PART, :].reshape(2 * H, H)
    wait(small_row.at[:3], recv_sem.at[SMALL_ROW])
    total = jnp.sum(small_row[...], 0) * (1.0 / N)
    gg_ref[...] = total[0:1]
    bg_ref[...] = total[1:2]
    wait(wholes.at[: SPOTS - 1], send_sem.at[WHOLE])
    wait(small_row.at[:3], send_sem.at[SMALL_ROW])


def deliver(a, b, c, d, out_a, out_b, out_c, out_d):
    out_a[...] = a[...]
    out_b[...] = b[...]
    out_c[...] = c[...]
    out_d[...] = d[...]


def local(pair_input, norm_gain, norm_bias, weights, cotangent):
    vmem = pl.BlockSpec(memory_space=pltpu.VMEM)
    results = (
        jax.ShapeDtypeStruct((PAIRS, H), BF16),
        jax.ShapeDtypeStruct((4 * H, H), F32),
        jax.ShapeDtypeStruct((1, H), F32),
        jax.ShapeDtypeStruct((1, H), F32),
    )
    computed = pl.pallas_call(
        kernel,
        out_shape=results,
        in_specs=[pl.BlockSpec(memory_space=pltpu.HBM)] * 5,
        out_specs=(vmem,) * 4,
        scratch_shapes=[
            pltpu.VMEM((PAIRS, H), BF16),
            pltpu.VMEM((1, H), F32),
            pltpu.VMEM((1, H), F32),
            pltpu.VMEM((4, H, H), BF16),
            pltpu.VMEM((PAIRS, H), BF16),
            pltpu.VMEM((PAIRS, 2 * W), F32),
            pltpu.VMEM((BAND, R, 2 * W), BF16),
            pltpu.VMEM((BAND, R, 2 * W), BF16),
            pltpu.VMEM((BAND, R, 2 * W), BF16),
            pltpu.VMEM((XS, YS, N, 2 * W), BF16),
            pltpu.VMEM((YS, N, 2 * W), BF16),
            pltpu.VMEM((YS, N, 2 * W), BF16),
            pltpu.VMEM((2 * N, YS * 2 * W), BF16),
            pltpu.VMEM((YS, N, 2 * W), BF16),
            pltpu.VMEM((YS, N, 2 * W), BF16),
            pltpu.VMEM((BAND, R, 2 * W), BF16),
            pltpu.VMEM((BAND, R, 2 * W), BF16),
            pltpu.VMEM((4 * H, PAIRS), F32),
            pltpu.VMEM((H, PAIRS), F32),
            pltpu.VMEM((H, PAIRS), BF16),
            pltpu.VMEM((R // 2, 2 * W), F32),
            pltpu.VMEM((4 * H, H), BF16),
            pltpu.VMEM((H, 4 * H), BF16),
            pltpu.VMEM((4 * H, PAIRS), BF16),
            pltpu.VMEM((H, PAIRS), F32),
            pltpu.VMEM((4 * H, H), F32),
            pltpu.VMEM((SPOTS, 2 * PART, H), F32),
            pltpu.VMEM((DEPTH, 2 * PART, H), F32),
            pltpu.VMEM((SPOTS, 2 * PART, H), F32),
            pltpu.VMEM((DEPTH, 8, H), F32),
            pltpu.VMEM((COLS, 8, H), F32),
            pltpu.VMEM((4, 8, H), F32),
            pltpu.SemaphoreType.DMA((13,)),
            pltpu.SemaphoreType.DMA((13,)),
            pltpu.SemaphoreType.DMA((XS, YS)),
            pltpu.SemaphoreType.DMA((5,)),
            pltpu.SemaphoreType.DMA((5,)),
        ],
        compiler_params=pltpu.CompilerParams(
            collective_id=0, has_side_effects=True, vmem_limit_bytes=60 * 1024 * 1024
        ),
        name="triangle_backward",
    )(
        pair_input.reshape(PAIRS, H),
        norm_gain.reshape(1, H),
        norm_bias.reshape(1, H),
        weights,
        cotangent.reshape(PAIRS, H),
    )
    out, weight_grad, gain_grad, bias_grad = pl.pallas_call(
        deliver,
        out_shape=results,
        in_specs=[vmem] * 4,
        out_specs=(vmem,) * 4,
        name="deliver",
    )(*computed)
    return (
        out.reshape(R, W, H),
        weight_grad.reshape(4, H, H),
        gain_grad.reshape(H),
        bias_grad.reshape(H),
    )


def solution(mesh):
    placed = (P("row", "col", None), P(), P(), P(), P("row", "col", None))
    return jax.shard_map(
        local,
        mesh=mesh,
        in_specs=placed,
        out_specs=(P("row", "col", None), P(), P(), P()),
        check_vma=False,
    )
```

```python
import jax
import jax.numpy as jnp
from jax import lax
from jax.experimental import pallas as pl
from jax.experimental.pallas import tpu as pltpu
from jax.sharding import PartitionSpec as P

MESH = pl.DeviceIdType.MESH
F32 = jnp.float32
BF16 = jnp.bfloat16

ROWS, COLS, DEPTH, XS, YS = 32, 8, 8, 4, 2
R, W, H, N = 16, 64, 128, 512
PAIRS = R * W
BAND = ROWS * YS
SPOTS = COLS * 4
PART = 4 * H // SPOTS // 2

COT, OP_FIRST, OP_SECOND, FIRST, SECOND, SMALL_Z, SMALL_COL, SMALL_ROW, RING = range(9)
PARTS, DEEPS, WHOLES = (9, 10), (11, 12), (13, 14)


def nt(a, b):
    return lax.dot_general(a, b, (((1,), (1,)), ((), ())), preferred_element_type=F32)


def tn(a, b):
    return lax.dot_general(a, b, (((0,), (0,)), ((), ())), preferred_element_type=F32)


def kernel(
    pair_hbm, gain_hbm, bias_hbm, w_hbm, cot_hbm,
    out_ref, wg_ref, gg_ref, bg_ref,
    pair_ref, gain_ref, bias_ref, w_ref, cot_ref,
    stage, send_cot, send_first, send_second, cots, firsts, seconds, blocks, out_first, out_second, got_first, got_second,
    factors, scaled, normed, inverse, w_t, w_cat, grads, normed_grad, w_part, parts, deeps, wholes, small_z, small_col, small_row,
    send_sem, recv_sem, cot_sem, ring_sem, local_sem, load_sem,
):
    row, col = lax.axis_index("row"), lax.axis_index("col")
    z, core, y_lo = lax.rem(row // 2, DEPTH), lax.rem(row, 2), row // (2 * DEPTH)
    x, y_hi = col // YS, lax.rem(col, YS)
    y = y_hi * 2 + y_lo
    plane = y_hi * ROWS + row

    loads = [
        pltpu.make_async_copy(src, dst, load_sem.at[i])
        for i, (src, dst) in enumerate(
            ((cot_hbm, cot_ref), (pair_hbm, pair_ref), (w_hbm, w_ref), (gain_hbm, gain_ref), (bias_hbm, bias_ref))
        )
    ]
    for load in loads:
        load.start()

    left_lanes = lax.broadcasted_iota(jnp.int32, (W, 2 * W), 1) < W
    eye = (
        lax.broadcasted_iota(jnp.int32, (H, H), 0) == lax.broadcasted_iota(jnp.int32, (H, H), 1)
    ).astype(F32).astype(BF16)

    def plane_row(s):
        return (s // 2) * (2 * DEPTH) + z * 2 + lax.rem(s, 2)

    def send(src, dst, kind, device, arrived=None):
        pltpu.make_async_remote_copy(
            src_ref=src,
            dst_ref=dst,
            send_sem=send_sem.at[kind],
            recv_sem=recv_sem.at[kind] if arrived is None else arrived,
            device_id=device,
            device_id_type=MESH,
        ).start()

    def wait(ref, sem):
        pltpu.make_async_copy(ref, ref, sem).wait()

    def rows_of(p):
        return pl.ds(pl.multiple_of(p * R, R), R)

    near = []
    for dy in (2, 1, 3, 0):
        other_y = lax.rem(y + dy, 4)
        for dc in (1, 0):
            near.append((other_y // 2, lax.rem(other_y, 2), lax.rem(core + dc, 2)))

    def each_of_band(act, group=near):
        offsets = [(there, low * (2 * DEPTH) + c) for there, low, c in group]

        @pl.loop(0, DEPTH - 1)
        def _(s):
            dz = DEPTH // 2 + ((s + 1) // 2) * (1 - 2 * lax.rem(s, 2))
            base = lax.rem(z + dz, DEPTH) * 2
            for there, offset in offsets:
                act(there, base + offset)

        for there, offset in offsets[:-1] if group[-1] is near[-1] else offsets:
            act(there, z * 2 + offset)

    barrier = pltpu.get_barrier_semaphore()
    right_x, left_x, far_x = lax.rem(x + 1, XS), lax.rem(x + XS - 1, XS), lax.rem(x + 2, XS)
    right, left = right_x * YS + y_hi, left_x * YS + y_hi

    def greet(there, p):
        pl.semaphore_signal(barrier, inc=1, device_id=(p, x * YS + there), device_id_type=MESH)

    each_of_band(greet)
    for to in (right, left):
        pl.semaphore_signal(barrier, inc=1, device_id=(row, to), device_id_type=MESH)

    def spread(t, value):
        low, high = value[:BAND], value[BAND:]
        stage[pl.ds(2 * t * BAND, BAND), :] = jnp.where(left_lanes, low, pltpu.roll(high, W, 1))
        stage[pl.ds((2 * t + 1) * BAND, BAND), :] = jnp.where(left_lanes, pltpu.roll(low, W, 1), high)

    def to_planes(planes):
        @pl.loop(0, BAND, unroll=8)
        def _(h):
            planes[h] = stage[pl.ds(h, R, stride=BAND), :].astype(BF16)

    def scatter(planes, dst, kind):
        def act(there, p):
            send(planes.at[there * ROWS + p], dst, kind, (p, x * YS + there))

        each_of_band(act)
        own = pltpu.make_async_copy(planes.at[plane], dst, local_sem.at[kind])
        own.start()
        return own

    loads[0].wait()
    for t in range(R // 2):
        spread(t, nt(eye, cot_ref[t * 2 * W : (t + 1) * 2 * W, :]))
    to_planes(send_cot)
    pl.semaphore_wait(barrier, BAND - 1 + 2)

    def send_cot_to(there, p):
        send(
            send_cot.at[there * ROWS + p], cots.at[x, y_hi, rows_of(row), :], COT, (p, x * YS + there), cot_sem.at[y]
        )

    for dy in (3, 1, 2, 0):
        each_of_band(send_cot_to, near[2 * dy : 2 * dy + 2])
    own_cot = pltpu.make_async_copy(send_cot.at[plane], cots.at[x, y_hi, rows_of(row), :], local_sem.at[COT])
    own_cot.start()

    for load in loads[1:]:
        load.wait()
    gain = jnp.transpose(jnp.broadcast_to(gain_ref[...], (H, H)))
    bias = jnp.transpose(jnp.broadcast_to(bias_ref[...], (H, H)))
    for m in range(4):
        w_t[m * H : (m + 1) * H, :] = jnp.transpose(w_ref[m].astype(F32)).astype(BF16)
        w_cat[:, m * H : (m + 1) * H] = w_ref[m]
    for t in range(R // 2):
        lanes = slice(t * 2 * W, (t + 1) * 2 * W)
        values = nt(eye, pair_ref[lanes, :])
        centred = values - jnp.mean(values, 0, keepdims=True)
        inv = lax.rsqrt(jnp.mean(centred * centred, 0, keepdims=True) + 1e-05)
        scale = centred * inv
        inverse[t : t + 1, :] = inv
        scaled[:, lanes] = scale
        normed[:, lanes] = (scale * gain + bias).astype(BF16)

    def gated(side, planes):
        for t in range(R // 2):
            lanes = slice(t * 2 * W, (t + 1) * 2 * W)
            pre = jnp.dot(w_t[2 * side * H : 2 * (side + 1) * H, :], normed[:, lanes], preferred_element_type=F32)
            gate, value = jax.nn.sigmoid(pre[:H]), pre[H:]
            product = gate * value
            factors[2 * side * H : (2 * side + 1) * H, lanes] = product * (1.0 - gate)
            factors[(2 * side + 1) * H : 2 * (side + 1) * H, lanes] = gate
            spread(t, product)
        to_planes(planes)

    pieces = [lax.rem(y + dy, 4) for dy in (0, 3, 1, 2)]

    def pass_on(at, g, to):
        piece = cots.at[at, g // 2, pl.ds(pl.multiple_of(lax.rem(g, 2) * (N // 2), N // 2), N // 2), :]
        send(piece, piece, RING, (row, to), ring_sem.at[at, g])

    def arrived(at, g):
        wait(cots.at[0, 0, : N // 2, :], ring_sem.at[at, g])

    def start_round(i):
        wait(send_cot.at[: BAND // 4 - (i == 0)], cot_sem.at[pieces[i]])
        pass_on(x, pieces[i], right)
        pass_on(x, pieces[i], left)

    gated(0, send_first)
    own_op_first = scatter(send_first, firsts.at[y_hi, rows_of(row), :], OP_FIRST)
    own_cot.wait()
    start_round(0)
    gated(1, send_second)
    own_op_second = scatter(send_second, seconds.at[y_hi, rows_of(row), :], OP_SECOND)
    start_round(1)
    start_round(2)
    arrived(left_x, pieces[0])
    pass_on(left_x, pieces[0], right)
    start_round(3)
    arrived(right_x, pieces[1])
    pass_on(right_x, pieces[1], left)
    arrived(left_x, pieces[2])
    pass_on(left_x, pieces[2], right)
    arrived(right_x, pieces[3])
    pass_on(right_x, pieces[3], left)

    own_op_first.wait()
    wait(send_first.at[: BAND - 1], recv_sem.at[OP_FIRST])
    def second_products(at):
        cot = jnp.concatenate([cots[at, 0], cots[at, 1]], 1)
        both = tn(cot, jnp.concatenate([firsts[0], firsts[1]], 1))
        for there in range(YS):
            lanes = slice(there * 2 * W, (there + 1) * 2 * W)
            for k in range(YS):
                out_second[there, pl.ds(pl.multiple_of((YS * at + k) * W, W), W), :] = jnp.where(
                    left_lanes, both[2 * k * W : (2 * k + 1) * W, lanes], both[(2 * k + 1) * W : 2 * (k + 1) * W, lanes]
                ).astype(BF16)

        @pl.loop(0, ROWS // XS)
        def _(d):
            p = at * (ROWS // XS) + d
            mate = 1 - y_hi
            send(out_second.at[mate, rows_of(p), :], got_second.at[plane], SECOND, (p, x * YS + mate))

            @pl.when(p != row)
            def _():
                send(out_second.at[y_hi, rows_of(p), :], got_second.at[plane], SECOND, (p, col))

            @pl.when(p == row)
            def _():
                copy = pltpu.make_async_copy(
                    out_second.at[y_hi, rows_of(p), :], got_second.at[plane], local_sem.at[SECOND]
                )
                copy.start()
                copy.wait()

    second_products(x)
    arrived(left_x, pieces[1])
    arrived(left_x, pieces[3])
    second_products(left_x)
    arrived(right_x, pieces[0])
    arrived(right_x, pieces[2])
    second_products(right_x)
    for i in range(4):
        arrived(far_x, pieces[i])
    second_products(far_x)

    own_op_second.wait()
    wait(send_second.at[: BAND - 1], recv_sem.at[OP_SECOND])
    for q in range(COLS):
        for there in range(YS):
            block = seconds[there, q * W : (q + 1) * W, :].astype(F32)
            lanes = slice(there * 2 * W, (there + 1) * 2 * W)
            blocks[q * 2 * W : q * 2 * W + W, lanes] = jnp.where(left_lanes, block, 0.0).astype(BF16)
            blocks[q * 2 * W + W : (q + 1) * 2 * W, lanes] = jnp.where(left_lanes, 0.0, block).astype(BF16)
    for half in range(2):
        rows = slice(half * N // 2, (half + 1) * N // 2)
        cot = jnp.concatenate([cots[q // YS, q % YS, rows] for q in range(COLS)], 1)
        term = jnp.dot(cot, blocks[...], preferred_element_type=F32)
        for there in range(YS):
            out_first[there, rows, :] = term[:, there * 2 * W : (there + 1) * 2 * W].astype(BF16)

    def return_first(there, p):
        send(out_first.at[there, rows_of(p), :], got_first.at[plane], FIRST, (p, x * YS + there))

    each_of_band(return_first)
    own_first = pltpu.make_async_copy(out_first.at[y_hi, rows_of(row), :], got_first.at[plane], local_sem.at[FIRST])
    own_first.start()

    def gather_in(side, got):
        @pl.loop(0, BAND, unroll=8)
        def _(h):
            stage[pl.ds(pl.multiple_of(h * R, R), R), :] = got[h].astype(F32)

        for t in range(R // 2):
            lanes = slice(t * 2 * W, (t + 1) * 2 * W)
            even = stage[pl.ds(2 * t, BAND, stride=R), :]
            odd = stage[pl.ds(2 * t + 1, BAND, stride=R), :]
            grad = jnp.concatenate(
                [
                    jnp.where(left_lanes, even, pltpu.roll(odd, W, 1)),
                    jnp.where(left_lanes, pltpu.roll(even, W, 1), odd),
                ],
                0,
            )
            for m in (2 * side, 2 * side + 1):
                grads[m * H : (m + 1) * H, lanes] = (grad * factors[m * H : (m + 1) * H, lanes]).astype(BF16)

    spot = (y_lo * 2 + core) * COLS + col

    def each_spot(act):
        beside = [((low * 2 + c) * COLS + there, low * (2 * DEPTH) + z * 2 + c, there) for there, low, c in near]

        def visit(there_x, spots):
            for g, p, there in spots:
                act(g + there_x * YS, (p, there_x * YS + there))

        for dx in (2, 1, 3):
            visit(lax.rem(x + dx, XS), beside)
        visit(x, beside[:-1])

    def z_peer(d):
        return (y_lo * 2 * DEPTH + lax.rem(z + d, DEPTH) * 2 + core, col)

    def mine(side):
        return slice(side * PART, (side + 1) * PART)

    def weight_part(side):
        part = nt(normed[...], grads[2 * side * H : 2 * (side + 1) * H, :])
        for m in range(2):
            w_part[(2 * side + m) * H : (2 * side + m + 1) * H, :] = part[:, m * H : (m + 1) * H]

        def share(g):
            return pl.ds(pl.multiple_of(2 * side * H + g * PART, PART), PART)

        each_spot(lambda g, device: send(w_part.at[share(g), :], parts.at[spot, mine(side), :], PARTS[side], device))
        parts[spot, mine(side), :] = w_part[share(spot), :]

    def weight_deep(side):
        wait(parts.at[: SPOTS - 1, :PART, :], recv_sem.at[PARTS[side]])
        deeps[z, mine(side), :] = jnp.sum(parts[:, mine(side), :], 0)
        own = deeps.at[z, mine(side), :]

        @pl.loop(1, DEPTH)
        def _(d):
            send(own, own, DEEPS[side], z_peer(d))

    def weight_whole(side):
        wait(deeps.at[: DEPTH - 1, :PART, :], recv_sem.at[DEEPS[side]])
        wholes[spot, mine(side), :] = jnp.sum(deeps[:, mine(side), :], 0) * (1.0 / N)
        own = wholes.at[spot, mine(side), :]
        each_spot(lambda g, device: send(own, own, WHOLES[side], device))

    wait(send_cot.at[: BAND - 1], recv_sem.at[SECOND])
    gather_in(1, got_second)
    weight_part(1)
    own_first.wait()
    wait(send_cot.at[: BAND - 1], recv_sem.at[FIRST])
    gather_in(0, got_first)
    weight_part(0)
    weight_deep(1)

    gain_sum = jnp.zeros((H, 2 * W), F32)
    bias_sum = jnp.zeros((H, 2 * W), F32)
    for t in range(R // 2):
        lanes = slice(t * 2 * W, (t + 1) * 2 * W)
        grad = jnp.dot(w_cat[...], grads[:, lanes], preferred_element_type=F32)
        normed_grad[:, lanes] = grad
        gain_sum += grad * scaled[:, lanes]
        bias_sum += grad
    gain_sum = jnp.sum(jnp.transpose(gain_sum), 0, keepdims=True)
    bias_sum = jnp.sum(jnp.transpose(bias_sum), 0, keepdims=True)
    small_z[z] = jnp.concatenate([gain_sum, bias_sum, jnp.zeros((6, H), F32)], 0)

    @pl.loop(1, DEPTH)
    def _(d):
        send(small_z.at[z], small_z.at[z], SMALL_Z, z_peer(d))

    weight_deep(0)
    weight_whole(1)

    for t in range(R // 2):
        lanes = slice(t * 2 * W, (t + 1) * 2 * W)
        scale = scaled[:, lanes]
        grad = normed_grad[:, lanes] * gain
        pair = inverse[t : t + 1, :] * (
            grad - jnp.mean(grad, 0, keepdims=True) - scale * jnp.mean(grad * scale, 0, keepdims=True)
        )
        out_ref[lanes, :] = jnp.transpose(pair).astype(BF16)

    wait(small_z.at[: DEPTH - 1], recv_sem.at[SMALL_Z])
    small_col[col] = jnp.sum(small_z[...], 0)

    @pl.loop(1, COLS)
    def _(d):
        send(small_col.at[col], small_col.at[col], SMALL_COL, (row, lax.rem(col + d, COLS)))

    weight_whole(0)

    wait(small_col.at[: COLS - 1], recv_sem.at[SMALL_COL])
    quarter = y_lo * 2 + core
    small_row[quarter] = jnp.sum(small_col[...], 0)

    @pl.loop(1, 4)
    def _(d):
        send(small_row.at[quarter], small_row.at[quarter], SMALL_ROW, (plane_row(lax.rem(quarter + d, 4)), col))

    for kind in (COT, OP_FIRST, OP_SECOND, FIRST, SECOND):
        wait(send_cot.at[: BAND - 1], send_sem.at[kind])
    wait(cots.at[: XS - 1], send_sem.at[RING])
    for side in range(2):
        wait(parts.at[: SPOTS - 1, :PART, :], send_sem.at[PARTS[side]])
        wait(deeps.at[: DEPTH - 1, :PART, :], send_sem.at[DEEPS[side]])
    wait(small_z.at[: DEPTH - 1], send_sem.at[SMALL_Z])
    wait(small_col.at[: COLS - 1], send_sem.at[SMALL_COL])

    wait(small_row.at[:3], recv_sem.at[SMALL_ROW])
    total = jnp.sum(small_row[...], 0) * (1.0 / N)
    gg_ref[...] = total[0:1]
    bg_ref[...] = total[1:2]
    for side in (1, 0):
        wait(wholes.at[: SPOTS - 1, :PART, :], recv_sem.at[WHOLES[side]])
        wg_ref[2 * side * H : 2 * (side + 1) * H, :] = wholes[:, mine(side), :].reshape(2 * H, H)
        wait(wholes.at[: SPOTS - 1, :PART, :], send_sem.at[WHOLES[side]])
    wait(small_row.at[:3], send_sem.at[SMALL_ROW])


def deliver(a, b, c, d, out_a, out_b, out_c, out_d):
    out_a[...] = a[...]
    out_b[...] = b[...]
    out_c[...] = c[...]
    out_d[...] = d[...]


def local(pair_input, norm_gain, norm_bias, weights, cotangent):
    vmem = pl.BlockSpec(memory_space=pltpu.VMEM)
    results = (
        jax.ShapeDtypeStruct((PAIRS, H), BF16),
        jax.ShapeDtypeStruct((4 * H, H), F32),
        jax.ShapeDtypeStruct((1, H), F32),
        jax.ShapeDtypeStruct((1, H), F32),
    )
    computed = pl.pallas_call(
        kernel,
        out_shape=results,
        in_specs=[pl.BlockSpec(memory_space=pltpu.HBM)] * 5,
        out_specs=(vmem,) * 4,
        scratch_shapes=[
            pltpu.VMEM((PAIRS, H), BF16),
            pltpu.VMEM((1, H), F32),
            pltpu.VMEM((1, H), F32),
            pltpu.VMEM((4, H, H), BF16),
            pltpu.VMEM((PAIRS, H), BF16),
            pltpu.VMEM((PAIRS, 2 * W), F32),
            pltpu.VMEM((BAND, R, 2 * W), BF16),
            pltpu.VMEM((BAND, R, 2 * W), BF16),
            pltpu.VMEM((BAND, R, 2 * W), BF16),
            pltpu.VMEM((XS, YS, N, 2 * W), BF16),
            pltpu.VMEM((YS, N, 2 * W), BF16),
            pltpu.VMEM((YS, N, 2 * W), BF16),
            pltpu.VMEM((2 * N, YS * 2 * W), BF16),
            pltpu.VMEM((YS, N, 2 * W), BF16),
            pltpu.VMEM((YS, N, 2 * W), BF16),
            pltpu.VMEM((BAND, R, 2 * W), BF16),
            pltpu.VMEM((BAND, R, 2 * W), BF16),
            pltpu.VMEM((4 * H, PAIRS), F32),
            pltpu.VMEM((H, PAIRS), F32),
            pltpu.VMEM((H, PAIRS), BF16),
            pltpu.VMEM((R // 2, 2 * W), F32),
            pltpu.VMEM((4 * H, H), BF16),
            pltpu.VMEM((H, 4 * H), BF16),
            pltpu.VMEM((4 * H, PAIRS), BF16),
            pltpu.VMEM((H, PAIRS), F32),
            pltpu.VMEM((4 * H, H), F32),
            pltpu.VMEM((SPOTS, 2 * PART, H), F32),
            pltpu.VMEM((DEPTH, 2 * PART, H), F32),
            pltpu.VMEM((SPOTS, 2 * PART, H), F32),
            pltpu.VMEM((DEPTH, 8, H), F32),
            pltpu.VMEM((COLS, 8, H), F32),
            pltpu.VMEM((4, 8, H), F32),
            pltpu.SemaphoreType.DMA((15,)),
            pltpu.SemaphoreType.DMA((15,)),
            pltpu.SemaphoreType.DMA((4,)),
            pltpu.SemaphoreType.DMA((XS, 4)),
            pltpu.SemaphoreType.DMA((5,)),
            pltpu.SemaphoreType.DMA((5,)),
        ],
        compiler_params=pltpu.CompilerParams(
            collective_id=0, has_side_effects=True, vmem_limit_bytes=40 * 1024 * 1024
        ),
        name="triangle_backward",
    )(
        *(
            pltpu.with_memory_space_constraint(a, pltpu.HBM)
            for a in (
                pair_input.reshape(PAIRS, H),
                norm_gain.reshape(1, H),
                norm_bias.reshape(1, H),
                weights,
                cotangent.reshape(PAIRS, H),
            )
        ),
    )
    out, weight_grad, gain_grad, bias_grad = pl.pallas_call(
        deliver,
        out_shape=results,
        in_specs=[vmem] * 4,
        out_specs=(vmem,) * 4,
        compiler_params=pltpu.CompilerParams(vmem_limit_bytes=4 * 1024 * 1024),
        name="deliver",
    )(*computed)
    return (
        out.reshape(R, W, H),
        weight_grad.reshape(4, H, H),
        gain_grad.reshape(H),
        bias_grad.reshape(H),
    )


def solution(mesh):
    placed = (P("row", "col", None), P(), P(), P(), P("row", "col", None))
    return jax.shard_map(
        local,
        mesh=mesh,
        in_specs=placed,
        out_specs=(P("row", "col", None), P(), P(), P()),
        check_vma=False,
    )
```

```python
import jax
import jax.numpy as jnp
from jax import lax
from jax.experimental import pallas as pl
from jax.experimental.pallas import tpu as pltpu
from jax.sharding import PartitionSpec as P

MESH = pl.DeviceIdType.MESH
F32 = jnp.float32
BF16 = jnp.bfloat16

ROWS, COLS, DEPTH, XS, YS = 32, 8, 8, 4, 2
R, W, H, N = 16, 64, 128, 512
PAIRS = R * W
BAND = ROWS * YS
SPOTS = COLS * 4
PART = 4 * H // SPOTS // 2

COT, OP_FIRST, OP_SECOND, FIRST, SECOND, SMALL_Z, SMALL_COL, SMALL_ROW, RING = range(9)
PARTS, DEEPS, WHOLES = (9, 10), (11, 12), (13, 14)


def nt(a, b):
    return lax.dot_general(a, b, (((1,), (1,)), ((), ())), preferred_element_type=F32)


def tn(a, b):
    return lax.dot_general(a, b, (((0,), (0,)), ((), ())), preferred_element_type=F32)


def kernel(
    pair_hbm, gain_hbm, bias_hbm, w_hbm, cot_hbm,
    out_ref, wg_ref, gg_ref, bg_ref,
    pair_ref, gain_ref, bias_ref, w_ref, cot_ref,
    stage, send_cot, send_first, send_second, cots, firsts, seconds, blocks, out_first, out_second, got_first, got_second,
    factors, scaled, normed, inverse, w_t, w_cat, grads, normed_grad, w_part, parts, deeps, wholes, small_z, small_col, small_row,
    send_sem, recv_sem, cot_sem, ring_sem, local_sem, load_sem, ready_sem,
):
    row, col = lax.axis_index("row"), lax.axis_index("col")
    z, core, y_lo = lax.rem(row // 2, DEPTH), lax.rem(row, 2), row // (2 * DEPTH)
    x, y_hi = col // YS, lax.rem(col, YS)
    y = y_hi * 2 + y_lo
    plane = y_hi * ROWS + row

    loads = [
        pltpu.make_async_copy(src, dst, load_sem.at[i])
        for i, (src, dst) in enumerate(
            ((cot_hbm, cot_ref), (pair_hbm, pair_ref), (w_hbm, w_ref), (gain_hbm, gain_ref), (bias_hbm, bias_ref))
        )
    ]
    for load in loads:
        load.start()

    left_lanes = lax.broadcasted_iota(jnp.int32, (W, 2 * W), 1) < W
    eye = (
        lax.broadcasted_iota(jnp.int32, (H, H), 0) == lax.broadcasted_iota(jnp.int32, (H, H), 1)
    ).astype(F32).astype(BF16)

    def plane_row(s):
        return (s // 2) * (2 * DEPTH) + z * 2 + lax.rem(s, 2)

    def send(src, dst, kind, device, arrived=None):
        pltpu.make_async_remote_copy(
            src_ref=src,
            dst_ref=dst,
            send_sem=send_sem.at[kind],
            recv_sem=recv_sem.at[kind] if arrived is None else arrived,
            device_id=device,
            device_id_type=MESH,
        ).start()

    def wait(ref, sem):
        pltpu.make_async_copy(ref, ref, sem).wait()

    def rows_of(p):
        return pl.ds(pl.multiple_of(p * R, R), R)

    near = []
    for dy in (2, 1, 3, 0):
        other_y = lax.rem(y + dy, 4)
        for dc in (1, 0):
            near.append((other_y // 2, lax.rem(other_y, 2), lax.rem(core + dc, 2)))

    def each_of_band(act, group=near):
        offsets = [(there, low * (2 * DEPTH) + c) for there, low, c in group]

        @pl.loop(0, DEPTH - 1)
        def _(s):
            dz = DEPTH // 2 + ((s + 1) // 2) * (1 - 2 * lax.rem(s, 2))
            base = lax.rem(z + dz, DEPTH) * 2
            for there, offset in offsets:
                act(there, base + offset)

        for there, offset in offsets[:-1] if group[-1] is near[-1] else offsets:
            act(there, z * 2 + offset)

    barrier = pltpu.get_barrier_semaphore()
    right_x, left_x, far_x = lax.rem(x + 1, XS), lax.rem(x + XS - 1, XS), lax.rem(x + 2, XS)
    right, left = right_x * YS + y_hi, left_x * YS + y_hi

    def greet(there, p):
        pl.semaphore_signal(barrier, inc=1, device_id=(p, x * YS + there), device_id_type=MESH)

    each_of_band(greet, near[6:])
    others_y = [(near[2 * i + 1][0], near[2 * i + 1][1] * (2 * DEPTH) + z * 2 + core) for i in range(3)]
    for there, p in others_y:
        greet(there, p)
    for to in (right, left):
        pl.semaphore_signal(barrier, inc=1, device_id=(row, to), device_id_type=MESH)

    def spread(t, value):
        low, high = value[:BAND], value[BAND:]
        stage[pl.ds(2 * t * BAND, BAND), :] = jnp.where(left_lanes, low, pltpu.roll(high, W, 1))
        stage[pl.ds((2 * t + 1) * BAND, BAND), :] = jnp.where(left_lanes, pltpu.roll(low, W, 1), high)

    def to_planes(planes):
        @pl.loop(0, BAND, unroll=8)
        def _(h):
            planes[h] = stage[pl.ds(h, R, stride=BAND), :].astype(BF16)

    def scatter(planes, dst, kind, group):
        def act(there, p):
            send(planes.at[there * ROWS + p], dst, kind, (p, x * YS + there))

        each_of_band(act, group)
        if group[-1] is not near[-1]:
            return None
        own = pltpu.make_async_copy(planes.at[plane], dst, local_sem.at[kind])
        own.start()
        return own

    loads[0].wait()
    for t in range(R // 2):
        spread(t, nt(eye, cot_ref[t * 2 * W : (t + 1) * 2 * W, :]))
    to_planes(send_cot)
    pl.semaphore_wait(barrier, BAND // 4 - 1 + 3 + 2)
    for there, p in others_y:
        pl.semaphore_signal(ready_sem, inc=1, device_id=(p, x * YS + there), device_id_type=MESH)

    def send_cot_to(there, p):
        send(
            send_cot.at[there * ROWS + p], cots.at[x, y_hi, rows_of(row), :], COT, (p, x * YS + there), cot_sem.at[y]
        )

    each_of_band(send_cot_to, near[6:])
    own_cot = pltpu.make_async_copy(send_cot.at[plane], cots.at[x, y_hi, rows_of(row), :], local_sem.at[COT])
    own_cot.start()

    for load in loads[1:]:
        load.wait()
    gain = jnp.transpose(jnp.broadcast_to(gain_ref[...], (H, H)))
    bias = jnp.transpose(jnp.broadcast_to(bias_ref[...], (H, H)))
    for m in range(4):
        w_t[m * H : (m + 1) * H, :] = jnp.transpose(w_ref[m].astype(F32)).astype(BF16)
        w_cat[:, m * H : (m + 1) * H] = w_ref[m]
    for t in range(R // 2):
        lanes = slice(t * 2 * W, (t + 1) * 2 * W)
        values = nt(eye, pair_ref[lanes, :])
        centred = values - jnp.mean(values, 0, keepdims=True)
        inv = lax.rsqrt(jnp.mean(centred * centred, 0, keepdims=True) + 1e-05)
        scale = centred * inv
        inverse[t : t + 1, :] = inv
        scaled[:, lanes] = scale
        normed[:, lanes] = (scale * gain + bias).astype(BF16)

    def gated(side, planes):
        for t in range(R // 2):
            lanes = slice(t * 2 * W, (t + 1) * 2 * W)
            pre = jnp.dot(w_t[2 * side * H : 2 * (side + 1) * H, :], normed[:, lanes], preferred_element_type=F32)
            gate, value = jax.nn.sigmoid(pre[:H]), pre[H:]
            product = gate * value
            factors[2 * side * H : (2 * side + 1) * H, lanes] = product * (1.0 - gate)
            factors[(2 * side + 1) * H : 2 * (side + 1) * H, lanes] = gate
            spread(t, product)
        to_planes(planes)

    pieces = [lax.rem(y + dy, 4) for dy in (0, 3, 1, 2)]

    def pass_on(at, g, to):
        piece = cots.at[at, g // 2, pl.ds(pl.multiple_of(lax.rem(g, 2) * (N // 2), N // 2), N // 2), :]
        send(piece, piece, RING, (row, to), ring_sem.at[at, g])

    def arrived(at, g):
        wait(cots.at[0, 0, : N // 2, :], ring_sem.at[at, g])

    def start_round(i):
        wait(send_cot.at[: BAND // 4 - (i == 0)], cot_sem.at[pieces[i]])
        pass_on(x, pieces[i], right)
        pass_on(x, pieces[i], left)

    gated(0, send_first)
    own_op_first = scatter(send_first, firsts.at[y_hi, rows_of(row), :], OP_FIRST, near[6:])
    pl.semaphore_wait(ready_sem, 3)
    for dy in (1, 2, 0):
        each_of_band(send_cot_to, near[2 * dy : 2 * dy + 2])
    scatter(send_first, firsts.at[y_hi, rows_of(row), :], OP_FIRST, near[:6])
    own_cot.wait()
    start_round(0)
    gated(1, send_second)
    own_op_second = scatter(send_second, seconds.at[y_hi, rows_of(row), :], OP_SECOND, near)
    start_round(1)
    start_round(2)
    arrived(left_x, pieces[0])
    pass_on(left_x, pieces[0], right)
    start_round(3)
    arrived(right_x, pieces[1])
    pass_on(right_x, pieces[1], left)
    arrived(left_x, pieces[2])
    pass_on(left_x, pieces[2], right)
    arrived(right_x, pieces[3])
    pass_on(right_x, pieces[3], left)

    own_op_first.wait()
    wait(send_first.at[: BAND - 1], recv_sem.at[OP_FIRST])
    def second_products(at):
        cot = jnp.concatenate([cots[at, 0], cots[at, 1]], 1)
        both = tn(cot, jnp.concatenate([firsts[0], firsts[1]], 1))
        for there in range(YS):
            lanes = slice(there * 2 * W, (there + 1) * 2 * W)
            for k in range(YS):
                out_second[there, pl.ds(pl.multiple_of((YS * at + k) * W, W), W), :] = jnp.where(
                    left_lanes, both[2 * k * W : (2 * k + 1) * W, lanes], both[(2 * k + 1) * W : 2 * (k + 1) * W, lanes]
                ).astype(BF16)

        @pl.loop(0, ROWS // XS)
        def _(d):
            p = at * (ROWS // XS) + d
            mate = 1 - y_hi
            send(out_second.at[mate, rows_of(p), :], got_second.at[plane], SECOND, (p, x * YS + mate))

            @pl.when(p != row)
            def _():
                send(out_second.at[y_hi, rows_of(p), :], got_second.at[plane], SECOND, (p, col))

            @pl.when(p == row)
            def _():
                copy = pltpu.make_async_copy(
                    out_second.at[y_hi, rows_of(p), :], got_second.at[plane], local_sem.at[SECOND]
                )
                copy.start()
                copy.wait()

    second_products(x)
    arrived(left_x, pieces[1])
    arrived(left_x, pieces[3])
    second_products(left_x)
    arrived(right_x, pieces[0])
    arrived(right_x, pieces[2])
    second_products(right_x)
    for i in range(4):
        arrived(far_x, pieces[i])
    second_products(far_x)

    own_op_second.wait()
    wait(send_second.at[: BAND - 1], recv_sem.at[OP_SECOND])
    for q in range(COLS):
        for there in range(YS):
            block = seconds[there, q * W : (q + 1) * W, :].astype(F32)
            lanes = slice(there * 2 * W, (there + 1) * 2 * W)
            blocks[q * 2 * W : q * 2 * W + W, lanes] = jnp.where(left_lanes, block, 0.0).astype(BF16)
            blocks[q * 2 * W + W : (q + 1) * 2 * W, lanes] = jnp.where(left_lanes, 0.0, block).astype(BF16)
    for half in range(2):
        rows = slice(half * N // 2, (half + 1) * N // 2)
        cot = jnp.concatenate([cots[q // YS, q % YS, rows] for q in range(COLS)], 1)
        term = jnp.dot(cot, blocks[...], preferred_element_type=F32)
        for there in range(YS):
            out_first[there, rows, :] = term[:, there * 2 * W : (there + 1) * 2 * W].astype(BF16)

    def return_first(there, p):
        send(out_first.at[there, rows_of(p), :], got_first.at[plane], FIRST, (p, x * YS + there))

    each_of_band(return_first)
    own_first = pltpu.make_async_copy(out_first.at[y_hi, rows_of(row), :], got_first.at[plane], local_sem.at[FIRST])
    own_first.start()

    def gather_in(side, got):
        @pl.loop(0, BAND, unroll=8)
        def _(h):
            stage[pl.ds(pl.multiple_of(h * R, R), R), :] = got[h].astype(F32)

        for t in range(R // 2):
            lanes = slice(t * 2 * W, (t + 1) * 2 * W)
            even = stage[pl.ds(2 * t, BAND, stride=R), :]
            odd = stage[pl.ds(2 * t + 1, BAND, stride=R), :]
            grad = jnp.concatenate(
                [
                    jnp.where(left_lanes, even, pltpu.roll(odd, W, 1)),
                    jnp.where(left_lanes, pltpu.roll(even, W, 1), odd),
                ],
                0,
            )
            for m in (2 * side, 2 * side + 1):
                grads[m * H : (m + 1) * H, lanes] = (grad * factors[m * H : (m + 1) * H, lanes]).astype(BF16)

    spot = (y_lo * 2 + core) * COLS + col

    def each_spot(act):
        beside = [((low * 2 + c) * COLS + there, low * (2 * DEPTH) + z * 2 + c, there) for there, low, c in near]

        def visit(there_x, spots):
            for g, p, there in spots:
                act(g + there_x * YS, (p, there_x * YS + there))

        for dx in (2, 1, 3):
            visit(lax.rem(x + dx, XS), beside)
        visit(x, beside[:-1])

    def z_peer(d):
        return (y_lo * 2 * DEPTH + lax.rem(z + d, DEPTH) * 2 + core, col)

    def mine(side):
        return slice(side * PART, (side + 1) * PART)

    def weight_part(side):
        part = nt(normed[...], grads[2 * side * H : 2 * (side + 1) * H, :])
        for m in range(2):
            w_part[(2 * side + m) * H : (2 * side + m + 1) * H, :] = part[:, m * H : (m + 1) * H]

        def share(g):
            return pl.ds(pl.multiple_of(2 * side * H + g * PART, PART), PART)

        each_spot(lambda g, device: send(w_part.at[share(g), :], parts.at[spot, mine(side), :], PARTS[side], device))
        parts[spot, mine(side), :] = w_part[share(spot), :]

    def weight_deep(side):
        wait(parts.at[: SPOTS - 1, :PART, :], recv_sem.at[PARTS[side]])
        deeps[z, mine(side), :] = jnp.sum(parts[:, mine(side), :], 0)
        own = deeps.at[z, mine(side), :]

        @pl.loop(1, DEPTH)
        def _(d):
            send(own, own, DEEPS[side], z_peer(d))

    def weight_whole(side):
        wait(deeps.at[: DEPTH - 1, :PART, :], recv_sem.at[DEEPS[side]])
        wholes[spot, mine(side), :] = jnp.sum(deeps[:, mine(side), :], 0) * (1.0 / N)
        own = wholes.at[spot, mine(side), :]
        each_spot(lambda g, device: send(own, own, WHOLES[side], device))

    wait(send_cot.at[: BAND - 1], recv_sem.at[SECOND])
    gather_in(1, got_second)
    weight_part(1)
    own_first.wait()
    wait(send_cot.at[: BAND - 1], recv_sem.at[FIRST])
    gather_in(0, got_first)
    weight_part(0)
    weight_deep(1)

    gain_sum = jnp.zeros((H, 2 * W), F32)
    bias_sum = jnp.zeros((H, 2 * W), F32)
    for t in range(R // 2):
        lanes = slice(t * 2 * W, (t + 1) * 2 * W)
        grad = jnp.dot(w_cat[...], grads[:, lanes], preferred_element_type=F32)
        normed_grad[:, lanes] = grad
        gain_sum += grad * scaled[:, lanes]
        bias_sum += grad
    gain_sum = jnp.sum(jnp.transpose(gain_sum), 0, keepdims=True)
    bias_sum = jnp.sum(jnp.transpose(bias_sum), 0, keepdims=True)
    small_z[z] = jnp.concatenate([gain_sum, bias_sum, jnp.zeros((6, H), F32)], 0)

    @pl.loop(1, DEPTH)
    def _(d):
        send(small_z.at[z], small_z.at[z], SMALL_Z, z_peer(d))

    weight_deep(0)
    weight_whole(1)

    for t in range(R // 2):
        lanes = slice(t * 2 * W, (t + 1) * 2 * W)
        scale = scaled[:, lanes]
        grad = normed_grad[:, lanes] * gain
        pair = inverse[t : t + 1, :] * (
            grad - jnp.mean(grad, 0, keepdims=True) - scale * jnp.mean(grad * scale, 0, keepdims=True)
        )
        out_ref[lanes, :] = jnp.transpose(pair).astype(BF16)

    wait(small_z.at[: DEPTH - 1], recv_sem.at[SMALL_Z])
    small_col[col] = jnp.sum(small_z[...], 0)

    @pl.loop(1, COLS)
    def _(d):
        send(small_col.at[col], small_col.at[col], SMALL_COL, (row, lax.rem(col + d, COLS)))

    weight_whole(0)

    wait(small_col.at[: COLS - 1], recv_sem.at[SMALL_COL])
    quarter = y_lo * 2 + core
    small_row[quarter] = jnp.sum(small_col[...], 0)

    @pl.loop(1, 4)
    def _(d):
        send(small_row.at[quarter], small_row.at[quarter], SMALL_ROW, (plane_row(lax.rem(quarter + d, 4)), col))

    for kind in (COT, OP_FIRST, OP_SECOND, FIRST, SECOND):
        wait(send_cot.at[: BAND - 1], send_sem.at[kind])
    wait(cots.at[: XS - 1], send_sem.at[RING])
    for side in range(2):
        wait(parts.at[: SPOTS - 1, :PART, :], send_sem.at[PARTS[side]])
        wait(deeps.at[: DEPTH - 1, :PART, :], send_sem.at[DEEPS[side]])
    wait(small_z.at[: DEPTH - 1], send_sem.at[SMALL_Z])
    wait(small_col.at[: COLS - 1], send_sem.at[SMALL_COL])

    wait(small_row.at[:3], recv_sem.at[SMALL_ROW])
    total = jnp.sum(small_row[...], 0) * (1.0 / N)
    gg_ref[...] = total[0:1]
    bg_ref[...] = total[1:2]
    for side in (1, 0):
        wait(wholes.at[: SPOTS - 1, :PART, :], recv_sem.at[WHOLES[side]])
        wg_ref[2 * side * H : 2 * (side + 1) * H, :] = wholes[:, mine(side), :].reshape(2 * H, H)
        wait(wholes.at[: SPOTS - 1, :PART, :], send_sem.at[WHOLES[side]])
    wait(small_row.at[:3], send_sem.at[SMALL_ROW])


def deliver(a, b, c, d, out_a, out_b, out_c, out_d):
    out_a[...] = a[...]
    out_b[...] = b[...]
    out_c[...] = c[...]
    out_d[...] = d[...]


def local(pair_input, norm_gain, norm_bias, weights, cotangent):
    vmem = pl.BlockSpec(memory_space=pltpu.VMEM)
    results = (
        jax.ShapeDtypeStruct((PAIRS, H), BF16),
        jax.ShapeDtypeStruct((4 * H, H), F32),
        jax.ShapeDtypeStruct((1, H), F32),
        jax.ShapeDtypeStruct((1, H), F32),
    )
    computed = pl.pallas_call(
        kernel,
        out_shape=results,
        in_specs=[pl.BlockSpec(memory_space=pltpu.HBM)] * 5,
        out_specs=(vmem,) * 4,
        scratch_shapes=[
            pltpu.VMEM((PAIRS, H), BF16),
            pltpu.VMEM((1, H), F32),
            pltpu.VMEM((1, H), F32),
            pltpu.VMEM((4, H, H), BF16),
            pltpu.VMEM((PAIRS, H), BF16),
            pltpu.VMEM((PAIRS, 2 * W), F32),
            pltpu.VMEM((BAND, R, 2 * W), BF16),
            pltpu.VMEM((BAND, R, 2 * W), BF16),
            pltpu.VMEM((BAND, R, 2 * W), BF16),
            pltpu.VMEM((XS, YS, N, 2 * W), BF16),
            pltpu.VMEM((YS, N, 2 * W), BF16),
            pltpu.VMEM((YS, N, 2 * W), BF16),
            pltpu.VMEM((2 * N, YS * 2 * W), BF16),
            pltpu.VMEM((YS, N, 2 * W), BF16),
            pltpu.VMEM((YS, N, 2 * W), BF16),
            pltpu.VMEM((BAND, R, 2 * W), BF16),
            pltpu.VMEM((BAND, R, 2 * W), BF16),
            pltpu.VMEM((4 * H, PAIRS), F32),
            pltpu.VMEM((H, PAIRS), F32),
            pltpu.VMEM((H, PAIRS), BF16),
            pltpu.VMEM((R // 2, 2 * W), F32),
            pltpu.VMEM((4 * H, H), BF16),
            pltpu.VMEM((H, 4 * H), BF16),
            pltpu.VMEM((4 * H, PAIRS), BF16),
            pltpu.VMEM((H, PAIRS), F32),
            pltpu.VMEM((4 * H, H), F32),
            pltpu.VMEM((SPOTS, 2 * PART, H), F32),
            pltpu.VMEM((DEPTH, 2 * PART, H), F32),
            pltpu.VMEM((SPOTS, 2 * PART, H), F32),
            pltpu.VMEM((DEPTH, 8, H), F32),
            pltpu.VMEM((COLS, 8, H), F32),
            pltpu.VMEM((4, 8, H), F32),
            pltpu.SemaphoreType.DMA((15,)),
            pltpu.SemaphoreType.DMA((15,)),
            pltpu.SemaphoreType.DMA((4,)),
            pltpu.SemaphoreType.DMA((XS, 4)),
            pltpu.SemaphoreType.DMA((5,)),
            pltpu.SemaphoreType.DMA((5,)),
            pltpu.SemaphoreType.REGULAR,
        ],
        compiler_params=pltpu.CompilerParams(
            collective_id=0, has_side_effects=True, vmem_limit_bytes=40 * 1024 * 1024
        ),
        name="triangle_backward",
    )(
        *(
            pltpu.with_memory_space_constraint(a, pltpu.HBM)
            for a in (
                pair_input.reshape(PAIRS, H),
                norm_gain.reshape(1, H),
                norm_bias.reshape(1, H),
                weights,
                cotangent.reshape(PAIRS, H),
            )
        ),
    )
    out, weight_grad, gain_grad, bias_grad = pl.pallas_call(
        deliver,
        out_shape=results,
        in_specs=[vmem] * 4,
        out_specs=(vmem,) * 4,
        compiler_params=pltpu.CompilerParams(vmem_limit_bytes=4 * 1024 * 1024),
        name="deliver",
    )(*computed)
    return (
        out.reshape(R, W, H),
        weight_grad.reshape(4, H, H),
        gain_grad.reshape(H),
        bias_grad.reshape(H),
    )


def solution(mesh):
    placed = (P("row", "col", None), P(), P(), P(), P("row", "col", None))
    return jax.shard_map(
        local,
        mesh=mesh,
        in_specs=placed,
        out_specs=(P("row", "col", None), P(), P(), P()),
        check_vma=False,
    )
```

```python
import jax
import jax.numpy as jnp
from jax import lax
from jax.experimental import pallas as pl
from jax.experimental.pallas import tpu as pltpu
from jax.sharding import PartitionSpec as P

MESH = pl.DeviceIdType.MESH
F32 = jnp.float32
BF16 = jnp.bfloat16

ROWS, COLS, DEPTH, XS, YS = 32, 8, 8, 4, 2
R, W, H, N = 16, 64, 128, 512
PAIRS = R * W
BAND = ROWS * YS
SPOTS = COLS * 4
PART = 4 * H // SPOTS // 2

COT, OP_FIRST, OP_SECOND, FIRST, SECOND, SMALL_Z, SMALL_COL, SMALL_ROW, RING = range(9)
PARTS, DEEPS, WHOLES = (9, 10), (11, 12), (13, 14)


def nt(a, b):
    return lax.dot_general(a, b, (((1,), (1,)), ((), ())), preferred_element_type=F32)


def tn(a, b):
    return lax.dot_general(a, b, (((0,), (0,)), ((), ())), preferred_element_type=F32)


def kernel(
    pair_hbm, gain_hbm, bias_hbm, w_hbm, cot_hbm,
    out_ref, wg_ref, gg_ref, bg_ref,
    pair_ref, gain_ref, bias_ref, w_ref, cot_ref,
    stage, send_cot, send_first, send_second, cots, firsts, seconds, blocks, out_first, out_second, got_first, got_second,
    factors, scaled, normed, inverse, w_t, w_cat, grads, normed_grad, w_part, parts, deeps, wholes, small_z, small_col, small_row,
    send_sem, recv_sem, cot_sem, ring_sem, local_sem, load_sem, ready_sem,
):
    row, col = lax.axis_index("row"), lax.axis_index("col")
    z, core, y_lo = lax.rem(row // 2, DEPTH), lax.rem(row, 2), row // (2 * DEPTH)
    x, y_hi = col // YS, lax.rem(col, YS)
    y = y_hi * 2 + y_lo
    plane = y_hi * ROWS + row

    loads = [
        pltpu.make_async_copy(src, dst, load_sem.at[i])
        for i, (src, dst) in enumerate(
            ((cot_hbm, cot_ref), (pair_hbm, pair_ref), (w_hbm, w_ref), (gain_hbm, gain_ref), (bias_hbm, bias_ref))
        )
    ]
    for load in loads:
        load.start()

    left_lanes = lax.broadcasted_iota(jnp.int32, (W, 2 * W), 1) < W
    eye = (
        lax.broadcasted_iota(jnp.int32, (H, H), 0) == lax.broadcasted_iota(jnp.int32, (H, H), 1)
    ).astype(F32).astype(BF16)

    def plane_row(s):
        return (s // 2) * (2 * DEPTH) + z * 2 + lax.rem(s, 2)

    def send(src, dst, kind, device, arrived=None):
        pltpu.make_async_remote_copy(
            src_ref=src,
            dst_ref=dst,
            send_sem=send_sem.at[kind],
            recv_sem=recv_sem.at[kind] if arrived is None else arrived,
            device_id=device,
            device_id_type=MESH,
        ).start()

    def wait(ref, sem):
        pltpu.make_async_copy(ref, ref, sem).wait()

    def rows_of(p):
        return pl.ds(pl.multiple_of(p * R, R), R)

    near = []
    for dy in (2, 1, 3, 0):
        other_y = lax.rem(y + dy, 4)
        for dc in (1, 0):
            near.append((other_y // 2, lax.rem(other_y, 2), lax.rem(core + dc, 2)))

    def each_of_band(act, group=near):
        offsets = [(there, low * (2 * DEPTH) + c) for there, low, c in group]

        @pl.loop(0, DEPTH - 1)
        def _(s):
            dz = DEPTH // 2 + ((s + 1) // 2) * (1 - 2 * lax.rem(s, 2))
            base = lax.rem(z + dz, DEPTH) * 2
            for there, offset in offsets:
                act(there, base + offset)

        for there, offset in offsets[:-1] if group[-1] is near[-1] else offsets:
            act(there, z * 2 + offset)

    barrier = pltpu.get_barrier_semaphore()
    right_x, left_x, far_x = lax.rem(x + 1, XS), lax.rem(x + XS - 1, XS), lax.rem(x + 2, XS)
    right, left = right_x * YS + y_hi, left_x * YS + y_hi

    def greet(there, p):
        pl.semaphore_signal(barrier, inc=1, device_id=(p, x * YS + there), device_id_type=MESH)

    each_of_band(greet, near[6:])
    others_y = [(near[2 * i + 1][0], near[2 * i + 1][1] * (2 * DEPTH) + z * 2 + core) for i in range(3)]
    for there, p in others_y:
        greet(there, p)
    for to in (right, left):
        pl.semaphore_signal(barrier, inc=1, device_id=(row, to), device_id_type=MESH)

    def spread(t, value):
        low, high = value[:BAND], value[BAND:]
        stage[pl.ds(2 * t * BAND, BAND), :] = jnp.where(left_lanes, low, pltpu.roll(high, W, 1))
        stage[pl.ds((2 * t + 1) * BAND, BAND), :] = jnp.where(left_lanes, pltpu.roll(low, W, 1), high)

    def to_planes(planes):
        @pl.loop(0, BAND, unroll=8)
        def _(h):
            planes[h] = stage[pl.ds(h, R, stride=BAND), :].astype(BF16)

    def scatter(planes, dst, kind, group):
        def act(there, p):
            send(planes.at[there * ROWS + p], dst, kind, (p, x * YS + there))

        each_of_band(act, group)
        if group[-1] is not near[-1]:
            return None
        own = pltpu.make_async_copy(planes.at[plane], dst, local_sem.at[kind])
        own.start()
        return own

    loads[0].wait()
    for t in range(R // 2):
        spread(t, nt(eye, cot_ref[t * 2 * W : (t + 1) * 2 * W, :]))
    to_planes(send_cot)
    pl.semaphore_wait(barrier, BAND // 4 - 1 + 3 + 2)
    for there, p in others_y:
        pl.semaphore_signal(ready_sem, inc=1, device_id=(p, x * YS + there), device_id_type=MESH)

    def send_cot_to(there, p):
        send(
            send_cot.at[there * ROWS + p], cots.at[x, y_hi, rows_of(row), :], COT, (p, x * YS + there), cot_sem.at[y]
        )

    each_of_band(send_cot_to, near[6:])
    own_cot = pltpu.make_async_copy(send_cot.at[plane], cots.at[x, y_hi, rows_of(row), :], local_sem.at[COT])
    own_cot.start()

    for load in loads[1:]:
        load.wait()
    gain = jnp.transpose(jnp.broadcast_to(gain_ref[...], (H, H)))
    bias = jnp.transpose(jnp.broadcast_to(bias_ref[...], (H, H)))
    for m in range(4):
        w_t[m * H : (m + 1) * H, :] = jnp.transpose(w_ref[m].astype(F32)).astype(BF16)
        w_cat[:, m * H : (m + 1) * H] = w_ref[m]
    for t in range(R // 2):
        lanes = slice(t * 2 * W, (t + 1) * 2 * W)
        values = nt(eye, pair_ref[lanes, :])
        centred = values - jnp.mean(values, 0, keepdims=True)
        inv = lax.rsqrt(jnp.mean(centred * centred, 0, keepdims=True) + 1e-05)
        scale = centred * inv
        inverse[t : t + 1, :] = inv
        scaled[:, lanes] = scale
        normed[:, lanes] = (scale * gain + bias).astype(BF16)

    def gated(side, planes):
        for t in range(R // 2):
            lanes = slice(t * 2 * W, (t + 1) * 2 * W)
            pre = jnp.dot(w_t[2 * side * H : 2 * (side + 1) * H, :], normed[:, lanes], preferred_element_type=F32)
            gate, value = jax.nn.sigmoid(pre[:H]), pre[H:]
            product = gate * value
            factors[2 * side * H : (2 * side + 1) * H, lanes] = product * (1.0 - gate)
            factors[(2 * side + 1) * H : 2 * (side + 1) * H, lanes] = gate
            spread(t, product)
        to_planes(planes)

    pieces = [lax.rem(y + dy, 4) for dy in (0, 3, 1, 2)]

    def pass_on(at, g, to):
        piece = cots.at[at, g // 2, pl.ds(pl.multiple_of(lax.rem(g, 2) * (N // 2), N // 2), N // 2), :]
        send(piece, piece, RING, (row, to), ring_sem.at[at, g])

    def arrived(at, g):
        wait(cots.at[0, 0, : N // 2, :], ring_sem.at[at, g])

    def start_round(i):
        wait(send_cot.at[: BAND // 4 - (i == 0)], cot_sem.at[pieces[i]])
        pass_on(x, pieces[i], right)
        pass_on(x, pieces[i], left)

    gated(0, send_first)
    own_op_first = scatter(send_first, firsts.at[y_hi, rows_of(row), :], OP_FIRST, near[6:])
    pl.semaphore_wait(ready_sem, 3)
    for dy in (1, 2, 0):
        each_of_band(send_cot_to, near[2 * dy : 2 * dy + 2])
    own_cot.wait()
    start_round(0)
    scatter(send_first, firsts.at[y_hi, rows_of(row), :], OP_FIRST, near[:6])
    gated(1, send_second)
    own_op_second = scatter(send_second, seconds.at[y_hi, rows_of(row), :], OP_SECOND, near)
    start_round(1)
    start_round(2)
    arrived(left_x, pieces[0])
    pass_on(left_x, pieces[0], right)
    start_round(3)
    arrived(right_x, pieces[1])
    pass_on(right_x, pieces[1], left)
    arrived(left_x, pieces[2])
    pass_on(left_x, pieces[2], right)
    arrived(right_x, pieces[3])
    pass_on(right_x, pieces[3], left)

    own_op_first.wait()
    wait(send_first.at[: BAND - 1], recv_sem.at[OP_FIRST])
    def second_products(at):
        cot = jnp.concatenate([cots[at, 0], cots[at, 1]], 1)
        both = tn(cot, jnp.concatenate([firsts[0], firsts[1]], 1))
        for there in range(YS):
            lanes = slice(there * 2 * W, (there + 1) * 2 * W)
            for k in range(YS):
                out_second[there, pl.ds(pl.multiple_of((YS * at + k) * W, W), W), :] = jnp.where(
                    left_lanes, both[2 * k * W : (2 * k + 1) * W, lanes], both[(2 * k + 1) * W : 2 * (k + 1) * W, lanes]
                ).astype(BF16)

        @pl.loop(0, ROWS // XS)
        def _(d):
            p = at * (ROWS // XS) + d
            mate = 1 - y_hi
            send(out_second.at[mate, rows_of(p), :], got_second.at[plane], SECOND, (p, x * YS + mate))

            @pl.when(p != row)
            def _():
                send(out_second.at[y_hi, rows_of(p), :], got_second.at[plane], SECOND, (p, col))

            @pl.when(p == row)
            def _():
                copy = pltpu.make_async_copy(
                    out_second.at[y_hi, rows_of(p), :], got_second.at[plane], local_sem.at[SECOND]
                )
                copy.start()
                copy.wait()

    second_products(x)
    arrived(left_x, pieces[1])
    arrived(left_x, pieces[3])
    second_products(left_x)
    arrived(right_x, pieces[0])
    arrived(right_x, pieces[2])
    second_products(right_x)
    for i in range(4):
        arrived(far_x, pieces[i])
    second_products(far_x)

    own_op_second.wait()
    wait(send_second.at[: BAND - 1], recv_sem.at[OP_SECOND])
    for q in range(COLS):
        for there in range(YS):
            block = seconds[there, q * W : (q + 1) * W, :].astype(F32)
            lanes = slice(there * 2 * W, (there + 1) * 2 * W)
            blocks[q * 2 * W : q * 2 * W + W, lanes] = jnp.where(left_lanes, block, 0.0).astype(BF16)
            blocks[q * 2 * W + W : (q + 1) * 2 * W, lanes] = jnp.where(left_lanes, 0.0, block).astype(BF16)
    for half in range(2):
        rows = slice(half * N // 2, (half + 1) * N // 2)
        cot = jnp.concatenate([cots[q // YS, q % YS, rows] for q in range(COLS)], 1)
        term = jnp.dot(cot, blocks[...], preferred_element_type=F32)
        for there in range(YS):
            out_first[there, rows, :] = term[:, there * 2 * W : (there + 1) * 2 * W].astype(BF16)

    def return_first(there, p):
        send(out_first.at[there, rows_of(p), :], got_first.at[plane], FIRST, (p, x * YS + there))

    each_of_band(return_first)
    own_first = pltpu.make_async_copy(out_first.at[y_hi, rows_of(row), :], got_first.at[plane], local_sem.at[FIRST])
    own_first.start()

    def gather_in(side, got):
        @pl.loop(0, BAND, unroll=8)
        def _(h):
            stage[pl.ds(pl.multiple_of(h * R, R), R), :] = got[h].astype(F32)

        for t in range(R // 2):
            lanes = slice(t * 2 * W, (t + 1) * 2 * W)
            even = stage[pl.ds(2 * t, BAND, stride=R), :]
            odd = stage[pl.ds(2 * t + 1, BAND, stride=R), :]
            grad = jnp.concatenate(
                [
                    jnp.where(left_lanes, even, pltpu.roll(odd, W, 1)),
                    jnp.where(left_lanes, pltpu.roll(even, W, 1), odd),
                ],
                0,
            )
            for m in (2 * side, 2 * side + 1):
                grads[m * H : (m + 1) * H, lanes] = (grad * factors[m * H : (m + 1) * H, lanes]).astype(BF16)

    spot = (y_lo * 2 + core) * COLS + col

    def each_spot(act):
        beside = [((low * 2 + c) * COLS + there, low * (2 * DEPTH) + z * 2 + c, there) for there, low, c in near]

        def visit(there_x, spots):
            for g, p, there in spots:
                act(g + there_x * YS, (p, there_x * YS + there))

        for dx in (2, 1, 3):
            visit(lax.rem(x + dx, XS), beside)
        visit(x, beside[:-1])

    def z_peer(d):
        return (y_lo * 2 * DEPTH + lax.rem(z + d, DEPTH) * 2 + core, col)

    def mine(side):
        return slice(side * PART, (side + 1) * PART)

    def weight_part(side):
        part = nt(normed[...], grads[2 * side * H : 2 * (side + 1) * H, :])
        for m in range(2):
            w_part[(2 * side + m) * H : (2 * side + m + 1) * H, :] = part[:, m * H : (m + 1) * H]

        def share(g):
            return pl.ds(pl.multiple_of(2 * side * H + g * PART, PART), PART)

        each_spot(lambda g, device: send(w_part.at[share(g), :], parts.at[spot, mine(side), :], PARTS[side], device))
        parts[spot, mine(side), :] = w_part[share(spot), :]

    def weight_deep(side):
        wait(parts.at[: SPOTS - 1, :PART, :], recv_sem.at[PARTS[side]])
        deeps[z, mine(side), :] = jnp.sum(parts[:, mine(side), :], 0)
        own = deeps.at[z, mine(side), :]

        @pl.loop(1, DEPTH)
        def _(d):
            send(own, own, DEEPS[side], z_peer(d))

    def weight_whole(side):
        wait(deeps.at[: DEPTH - 1, :PART, :], recv_sem.at[DEEPS[side]])
        wholes[spot, mine(side), :] = jnp.sum(deeps[:, mine(side), :], 0) * (1.0 / N)
        own = wholes.at[spot, mine(side), :]
        each_spot(lambda g, device: send(own, own, WHOLES[side], device))

    wait(send_cot.at[: BAND - 1], recv_sem.at[SECOND])
    gather_in(1, got_second)
    weight_part(1)
    own_first.wait()
    wait(send_cot.at[: BAND - 1], recv_sem.at[FIRST])
    gather_in(0, got_first)
    weight_part(0)
    weight_deep(1)

    gain_sum = jnp.zeros((H, 2 * W), F32)
    bias_sum = jnp.zeros((H, 2 * W), F32)
    for t in range(R // 2):
        lanes = slice(t * 2 * W, (t + 1) * 2 * W)
        grad = jnp.dot(w_cat[...], grads[:, lanes], preferred_element_type=F32)
        normed_grad[:, lanes] = grad
        gain_sum += grad * scaled[:, lanes]
        bias_sum += grad
    gain_sum = jnp.sum(jnp.transpose(gain_sum), 0, keepdims=True)
    bias_sum = jnp.sum(jnp.transpose(bias_sum), 0, keepdims=True)
    small_z[z] = jnp.concatenate([gain_sum, bias_sum, jnp.zeros((6, H), F32)], 0)

    @pl.loop(1, DEPTH)
    def _(d):
        send(small_z.at[z], small_z.at[z], SMALL_Z, z_peer(d))

    weight_deep(0)
    weight_whole(1)

    for t in range(R // 2):
        lanes = slice(t * 2 * W, (t + 1) * 2 * W)
        scale = scaled[:, lanes]
        grad = normed_grad[:, lanes] * gain
        pair = inverse[t : t + 1, :] * (
            grad - jnp.mean(grad, 0, keepdims=True) - scale * jnp.mean(grad * scale, 0, keepdims=True)
        )
        out_ref[lanes, :] = jnp.transpose(pair).astype(BF16)

    wait(small_z.at[: DEPTH - 1], recv_sem.at[SMALL_Z])
    small_col[col] = jnp.sum(small_z[...], 0)

    @pl.loop(1, COLS)
    def _(d):
        send(small_col.at[col], small_col.at[col], SMALL_COL, (row, lax.rem(col + d, COLS)))

    weight_whole(0)

    wait(small_col.at[: COLS - 1], recv_sem.at[SMALL_COL])
    quarter = y_lo * 2 + core
    small_row[quarter] = jnp.sum(small_col[...], 0)

    @pl.loop(1, 4)
    def _(d):
        send(small_row.at[quarter], small_row.at[quarter], SMALL_ROW, (plane_row(lax.rem(quarter + d, 4)), col))

    for kind in (COT, OP_FIRST, OP_SECOND, FIRST, SECOND):
        wait(send_cot.at[: BAND - 1], send_sem.at[kind])
    wait(cots.at[: XS - 1], send_sem.at[RING])
    for side in range(2):
        wait(parts.at[: SPOTS - 1, :PART, :], send_sem.at[PARTS[side]])
        wait(deeps.at[: DEPTH - 1, :PART, :], send_sem.at[DEEPS[side]])
    wait(small_z.at[: DEPTH - 1], send_sem.at[SMALL_Z])
    wait(small_col.at[: COLS - 1], send_sem.at[SMALL_COL])

    wait(small_row.at[:3], recv_sem.at[SMALL_ROW])
    total = jnp.sum(small_row[...], 0) * (1.0 / N)
    gg_ref[...] = total[0:1]
    bg_ref[...] = total[1:2]
    for side in (1, 0):
        wait(wholes.at[: SPOTS - 1, :PART, :], recv_sem.at[WHOLES[side]])
        wg_ref[2 * side * H : 2 * (side + 1) * H, :] = wholes[:, mine(side), :].reshape(2 * H, H)
        wait(wholes.at[: SPOTS - 1, :PART, :], send_sem.at[WHOLES[side]])
    wait(small_row.at[:3], send_sem.at[SMALL_ROW])


def deliver(a, b, c, d, out_a, out_b, out_c, out_d):
    out_a[...] = a[...]
    out_b[...] = b[...]
    out_c[...] = c[...]
    out_d[...] = d[...]


def local(pair_input, norm_gain, norm_bias, weights, cotangent):
    vmem = pl.BlockSpec(memory_space=pltpu.VMEM)
    results = (
        jax.ShapeDtypeStruct((PAIRS, H), BF16),
        jax.ShapeDtypeStruct((4 * H, H), F32),
        jax.ShapeDtypeStruct((1, H), F32),
        jax.ShapeDtypeStruct((1, H), F32),
    )
    computed = pl.pallas_call(
        kernel,
        out_shape=results,
        in_specs=[pl.BlockSpec(memory_space=pltpu.HBM)] * 5,
        out_specs=(vmem,) * 4,
        scratch_shapes=[
            pltpu.VMEM((PAIRS, H), BF16),
            pltpu.VMEM((1, H), F32),
            pltpu.VMEM((1, H), F32),
            pltpu.VMEM((4, H, H), BF16),
            pltpu.VMEM((PAIRS, H), BF16),
            pltpu.VMEM((PAIRS, 2 * W), F32),
            pltpu.VMEM((BAND, R, 2 * W), BF16),
            pltpu.VMEM((BAND, R, 2 * W), BF16),
            pltpu.VMEM((BAND, R, 2 * W), BF16),
            pltpu.VMEM((XS, YS, N, 2 * W), BF16),
            pltpu.VMEM((YS, N, 2 * W), BF16),
            pltpu.VMEM((YS, N, 2 * W), BF16),
            pltpu.VMEM((2 * N, YS * 2 * W), BF16),
            pltpu.VMEM((YS, N, 2 * W), BF16),
            pltpu.VMEM((YS, N, 2 * W), BF16),
            pltpu.VMEM((BAND, R, 2 * W), BF16),
            pltpu.VMEM((BAND, R, 2 * W), BF16),
            pltpu.VMEM((4 * H, PAIRS), F32),
            pltpu.VMEM((H, PAIRS), F32),
            pltpu.VMEM((H, PAIRS), BF16),
            pltpu.VMEM((R // 2, 2 * W), F32),
            pltpu.VMEM((4 * H, H), BF16),
            pltpu.VMEM((H, 4 * H), BF16),
            pltpu.VMEM((4 * H, PAIRS), BF16),
            pltpu.VMEM((H, PAIRS), F32),
            pltpu.VMEM((4 * H, H), F32),
            pltpu.VMEM((SPOTS, 2 * PART, H), F32),
            pltpu.VMEM((DEPTH, 2 * PART, H), F32),
            pltpu.VMEM((SPOTS, 2 * PART, H), F32),
            pltpu.VMEM((DEPTH, 8, H), F32),
            pltpu.VMEM((COLS, 8, H), F32),
            pltpu.VMEM((4, 8, H), F32),
            pltpu.SemaphoreType.DMA((15,)),
            pltpu.SemaphoreType.DMA((15,)),
            pltpu.SemaphoreType.DMA((4,)),
            pltpu.SemaphoreType.DMA((XS, 4)),
            pltpu.SemaphoreType.DMA((5,)),
            pltpu.SemaphoreType.DMA((5,)),
            pltpu.SemaphoreType.REGULAR,
        ],
        compiler_params=pltpu.CompilerParams(
            collective_id=0, has_side_effects=True, vmem_limit_bytes=40 * 1024 * 1024
        ),
        name="triangle_backward",
    )(
        *(
            pltpu.with_memory_space_constraint(a, pltpu.HBM)
            for a in (
                pair_input.reshape(PAIRS, H),
                norm_gain.reshape(1, H),
                norm_bias.reshape(1, H),
                weights,
                cotangent.reshape(PAIRS, H),
            )
        ),
    )
    out, weight_grad, gain_grad, bias_grad = pl.pallas_call(
        deliver,
        out_shape=results,
        in_specs=[vmem] * 4,
        out_specs=(vmem,) * 4,
        compiler_params=pltpu.CompilerParams(vmem_limit_bytes=4 * 1024 * 1024),
        name="deliver",
    )(*computed)
    return (
        out.reshape(R, W, H),
        weight_grad.reshape(4, H, H),
        gain_grad.reshape(H),
        bias_grad.reshape(H),
    )


def solution(mesh):
    placed = (P("row", "col", None), P(), P(), P(), P("row", "col", None))
    return jax.shard_map(
        local,
        mesh=mesh,
        in_specs=placed,
        out_specs=(P("row", "col", None), P(), P(), P()),
        check_vma=False,
    )
```

```python
import jax
import jax.numpy as jnp
from jax import lax
from jax.experimental import pallas as pl
from jax.experimental.pallas import tpu as pltpu
from jax.sharding import PartitionSpec as P

MESH = pl.DeviceIdType.MESH
F32 = jnp.float32
BF16 = jnp.bfloat16

ROWS, COLS, DEPTH, XS, YS = 32, 8, 8, 4, 2
R, W, H, N = 16, 64, 128, 512
PAIRS = R * W
BAND = ROWS * YS
SPOTS = COLS * 4
PART = 4 * H // SPOTS // 2

COT, OP_FIRST, OP_SECOND, FIRST, SECOND, SMALL_Z, SMALL_COL, SMALL_ROW, RING = range(9)
PARTS, DEEPS, WHOLES = (9, 10), (11, 12), (13, 14)


def nt(a, b):
    return lax.dot_general(a, b, (((1,), (1,)), ((), ())), preferred_element_type=F32)


def tn(a, b):
    return lax.dot_general(a, b, (((0,), (0,)), ((), ())), preferred_element_type=F32)


def kernel(
    pair_hbm, gain_hbm, bias_hbm, w_hbm, cot_hbm,
    out_ref, wg_ref, gg_ref, bg_ref,
    pair_ref, gain_ref, bias_ref, w_ref, cot_ref,
    stage, send_cot, send_first, send_second, cots, firsts, seconds, blocks, out_first, out_second, got_first, got_second,
    factors, scaled, normed, inverse, w_t, w_cat, grads, normed_grad, w_part, parts, deeps, wholes, small_z, small_col, small_row,
    send_sem, recv_sem, cot_sem, ring_sem, local_sem, load_sem, ready_sem,
):
    row, col = lax.axis_index("row"), lax.axis_index("col")
    z, core, y_lo = lax.rem(row // 2, DEPTH), lax.rem(row, 2), row // (2 * DEPTH)
    x, y_hi = col // YS, lax.rem(col, YS)
    y = y_hi * 2 + y_lo
    plane = y_hi * ROWS + row

    loads = [
        pltpu.make_async_copy(src, dst, load_sem.at[i])
        for i, (src, dst) in enumerate(
            ((cot_hbm, cot_ref), (pair_hbm, pair_ref), (w_hbm, w_ref), (gain_hbm, gain_ref), (bias_hbm, bias_ref))
        )
    ]
    for load in loads:
        load.start()

    left_lanes = lax.broadcasted_iota(jnp.int32, (W, 2 * W), 1) < W
    eye = (
        lax.broadcasted_iota(jnp.int32, (H, H), 0) == lax.broadcasted_iota(jnp.int32, (H, H), 1)
    ).astype(F32).astype(BF16)

    def plane_row(s):
        return (s // 2) * (2 * DEPTH) + z * 2 + lax.rem(s, 2)

    def send(src, dst, kind, device, arrived=None):
        pltpu.make_async_remote_copy(
            src_ref=src,
            dst_ref=dst,
            send_sem=send_sem.at[kind],
            recv_sem=recv_sem.at[kind] if arrived is None else arrived,
            device_id=device,
            device_id_type=MESH,
        ).start()

    def wait(ref, sem):
        pltpu.make_async_copy(ref, ref, sem).wait()

    def rows_of(p):
        return pl.ds(pl.multiple_of(p * R, R), R)

    near = []
    for dy in (2, 1, 3, 0):
        other_y = lax.rem(y + dy, 4)
        for dc in (1, 0):
            near.append((other_y // 2, lax.rem(other_y, 2), lax.rem(core + dc, 2)))

    def each_of_band(act, group=near):
        offsets = [(there, low * (2 * DEPTH) + c) for there, low, c in group]

        @pl.loop(0, DEPTH - 1)
        def _(s):
            dz = DEPTH // 2 + ((s + 1) // 2) * (1 - 2 * lax.rem(s, 2))
            base = lax.rem(z + dz, DEPTH) * 2
            for there, offset in offsets:
                act(there, base + offset)

        for there, offset in offsets[:-1] if group[-1] is near[-1] else offsets:
            act(there, z * 2 + offset)

    barrier = pltpu.get_barrier_semaphore()
    right_x, left_x, far_x = lax.rem(x + 1, XS), lax.rem(x + XS - 1, XS), lax.rem(x + 2, XS)
    right, left = right_x * YS + y_hi, left_x * YS + y_hi

    def greet(there, p):
        pl.semaphore_signal(barrier, inc=1, device_id=(p, x * YS + there), device_id_type=MESH)

    each_of_band(greet, near[6:])
    others_y = [(near[2 * i + 1][0], near[2 * i + 1][1] * (2 * DEPTH) + z * 2 + core) for i in range(3)]
    for there, p in others_y:
        greet(there, p)
    for to in (right, left):
        pl.semaphore_signal(barrier, inc=1, device_id=(row, to), device_id_type=MESH)

    def spread(t, value):
        low, high = value[:BAND], value[BAND:]
        stage[pl.ds(2 * t * BAND, BAND), :] = jnp.where(left_lanes, low, pltpu.roll(high, W, 1))
        stage[pl.ds((2 * t + 1) * BAND, BAND), :] = jnp.where(left_lanes, pltpu.roll(low, W, 1), high)

    def to_planes(planes):
        @pl.loop(0, BAND, unroll=8)
        def _(h):
            planes[h] = stage[pl.ds(h, R, stride=BAND), :].astype(BF16)

    def scatter(planes, dst, kind, group):
        def act(there, p):
            send(planes.at[there * ROWS + p], dst, kind, (p, x * YS + there))

        each_of_band(act, group)
        if group[-1] is not near[-1]:
            return None
        own = pltpu.make_async_copy(planes.at[plane], dst, local_sem.at[kind])
        own.start()
        return own

    loads[0].wait()
    for t in range(R // 2):
        spread(t, nt(eye, cot_ref[t * 2 * W : (t + 1) * 2 * W, :]))
    to_planes(send_cot)
    pl.semaphore_wait(barrier, BAND // 4 - 1 + 3 + 2)
    for there, p in others_y:
        pl.semaphore_signal(ready_sem, inc=1, device_id=(p, x * YS + there), device_id_type=MESH)

    def send_cot_to(there, p):
        send(
            send_cot.at[there * ROWS + p], cots.at[x, y_hi, rows_of(row), :], COT, (p, x * YS + there), cot_sem.at[y]
        )

    each_of_band(send_cot_to, near[6:])
    own_cot = pltpu.make_async_copy(send_cot.at[plane], cots.at[x, y_hi, rows_of(row), :], local_sem.at[COT])
    own_cot.start()

    for load in loads[1:]:
        load.wait()
    gain = jnp.transpose(jnp.broadcast_to(gain_ref[...], (H, H)))
    bias = jnp.transpose(jnp.broadcast_to(bias_ref[...], (H, H)))
    for m in range(4):
        w_t[m * H : (m + 1) * H, :] = jnp.transpose(w_ref[m].astype(F32)).astype(BF16)
        w_cat[:, m * H : (m + 1) * H] = w_ref[m]
    for t in range(R // 2):
        lanes = slice(t * 2 * W, (t + 1) * 2 * W)
        values = nt(eye, pair_ref[lanes, :])
        centred = values - jnp.mean(values, 0, keepdims=True)
        inv = lax.rsqrt(jnp.mean(centred * centred, 0, keepdims=True) + 1e-05)
        scale = centred * inv
        inverse[t : t + 1, :] = inv
        scaled[:, lanes] = scale
        normed[:, lanes] = (scale * gain + bias).astype(BF16)

    def gated(side, planes):
        for t in range(R // 2):
            lanes = slice(t * 2 * W, (t + 1) * 2 * W)
            pre = jnp.dot(w_t[2 * side * H : 2 * (side + 1) * H, :], normed[:, lanes], preferred_element_type=F32)
            gate, value = jax.nn.sigmoid(pre[:H]), pre[H:]
            product = gate * value
            factors[2 * side * H : (2 * side + 1) * H, lanes] = product * (1.0 - gate)
            factors[(2 * side + 1) * H : 2 * (side + 1) * H, lanes] = gate
            spread(t, product)
        to_planes(planes)

    pieces = [lax.rem(y + dy, 4) for dy in (0, 3, 1, 2)]

    def pass_on(at, g, to):
        piece = cots.at[at, g // 2, pl.ds(pl.multiple_of(lax.rem(g, 2) * (N // 2), N // 2), N // 2), :]
        send(piece, piece, RING, (row, to), ring_sem.at[at, g])

    def arrived(at, g):
        wait(cots.at[0, 0, : N // 2, :], ring_sem.at[at, g])

    def start_round(i):
        wait(send_cot.at[: BAND // 4 - (i == 0)], cot_sem.at[pieces[i]])
        pass_on(x, pieces[i], right)
        pass_on(x, pieces[i], left)

    gated(0, send_first)
    own_op_first = scatter(send_first, firsts.at[y_hi, rows_of(row), :], OP_FIRST, near[6:])
    pl.semaphore_wait(ready_sem, 3)
    for dy in (1, 2, 0):
        each_of_band(send_cot_to, near[2 * dy : 2 * dy + 2])
    scatter(send_first, firsts.at[y_hi, rows_of(row), :], OP_FIRST, near[:6])
    own_cot.wait()
    start_round(0)
    gated(1, send_second)
    own_op_second = scatter(send_second, seconds.at[y_hi, rows_of(row), :], OP_SECOND, near)
    start_round(1)
    start_round(2)
    arrived(left_x, pieces[0])
    pass_on(left_x, pieces[0], right)
    start_round(3)
    arrived(right_x, pieces[1])
    pass_on(right_x, pieces[1], left)
    arrived(left_x, pieces[2])
    pass_on(left_x, pieces[2], right)
    arrived(right_x, pieces[3])
    pass_on(right_x, pieces[3], left)

    own_op_first.wait()
    wait(send_first.at[: BAND - 1], recv_sem.at[OP_FIRST])
    def second_products(at):
        cot = jnp.concatenate([cots[at, 0], cots[at, 1]], 1)
        both = tn(cot, jnp.concatenate([firsts[0], firsts[1]], 1))
        for there in range(YS):
            lanes = slice(there * 2 * W, (there + 1) * 2 * W)
            for k in range(YS):
                out_second[there, pl.ds(pl.multiple_of((YS * at + k) * W, W), W), :] = jnp.where(
                    left_lanes, both[2 * k * W : (2 * k + 1) * W, lanes], both[(2 * k + 1) * W : 2 * (k + 1) * W, lanes]
                ).astype(BF16)

        @pl.loop(0, ROWS // XS)
        def _(d):
            p = at * (ROWS // XS) + d
            mate = 1 - y_hi
            send(out_second.at[mate, rows_of(p), :], got_second.at[plane], SECOND, (p, x * YS + mate))

            @pl.when(p != row)
            def _():
                send(out_second.at[y_hi, rows_of(p), :], got_second.at[plane], SECOND, (p, col))

            @pl.when(p == row)
            def _():
                copy = pltpu.make_async_copy(
                    out_second.at[y_hi, rows_of(p), :], got_second.at[plane], local_sem.at[SECOND]
                )
                copy.start()
                copy.wait()

    second_products(x)
    arrived(left_x, pieces[1])
    arrived(left_x, pieces[3])
    second_products(left_x)
    arrived(right_x, pieces[0])
    arrived(right_x, pieces[2])
    second_products(right_x)
    for i in range(4):
        arrived(far_x, pieces[i])
    second_products(far_x)

    own_op_second.wait()
    wait(send_second.at[: BAND - 1], recv_sem.at[OP_SECOND])
    for q in range(COLS):
        for there in range(YS):
            block = seconds[there, q * W : (q + 1) * W, :].astype(F32)
            lanes = slice(there * 2 * W, (there + 1) * 2 * W)
            blocks[q * 2 * W : q * 2 * W + W, lanes] = jnp.where(left_lanes, block, 0.0).astype(BF16)
            blocks[q * 2 * W + W : (q + 1) * 2 * W, lanes] = jnp.where(left_lanes, 0.0, block).astype(BF16)
    for half in range(2):
        rows = slice(half * N // 2, (half + 1) * N // 2)
        cot = jnp.concatenate([cots[q // YS, q % YS, rows] for q in range(COLS)], 1)
        term = jnp.dot(cot, blocks[...], preferred_element_type=F32)
        for there in range(YS):
            out_first[there, rows, :] = term[:, there * 2 * W : (there + 1) * 2 * W].astype(BF16)

    def return_first(there, p):
        send(out_first.at[there, rows_of(p), :], got_first.at[plane], FIRST, (p, x * YS + there))

    each_of_band(return_first)
    own_first = pltpu.make_async_copy(out_first.at[y_hi, rows_of(row), :], got_first.at[plane], local_sem.at[FIRST])
    own_first.start()

    def gather_in(side, got):
        @pl.loop(0, BAND, unroll=8)
        def _(h):
            stage[pl.ds(pl.multiple_of(h * R, R), R), :] = got[h].astype(F32)

        for t in range(R // 2):
            lanes = slice(t * 2 * W, (t + 1) * 2 * W)
            even = stage[pl.ds(2 * t, BAND, stride=R), :]
            odd = stage[pl.ds(2 * t + 1, BAND, stride=R), :]
            grad = jnp.concatenate(
                [
                    jnp.where(left_lanes, even, pltpu.roll(odd, W, 1)),
                    jnp.where(left_lanes, pltpu.roll(even, W, 1), odd),
                ],
                0,
            )
            for m in (2 * side, 2 * side + 1):
                grads[m * H : (m + 1) * H, lanes] = (grad * factors[m * H : (m + 1) * H, lanes]).astype(BF16)

    spot = (y_lo * 2 + core) * COLS + col

    def each_spot(act):
        beside = [((low * 2 + c) * COLS + there, low * (2 * DEPTH) + z * 2 + c, there) for there, low, c in near]

        def visit(there_x, spots):
            for g, p, there in spots:
                act(g + there_x * YS, (p, there_x * YS + there))

        for dx in (2, 1, 3):
            visit(lax.rem(x + dx, XS), beside)
        visit(x, beside[:-1])

    def z_peer(d):
        return (y_lo * 2 * DEPTH + lax.rem(z + d, DEPTH) * 2 + core, col)

    def mine(side):
        return slice(side * PART, (side + 1) * PART)

    def weight_part(side):
        part = nt(normed[...], grads[2 * side * H : 2 * (side + 1) * H, :])
        for m in range(2):
            w_part[(2 * side + m) * H : (2 * side + m + 1) * H, :] = part[:, m * H : (m + 1) * H]

        def share(g):
            return pl.ds(pl.multiple_of(2 * side * H + g * PART, PART), PART)

        each_spot(lambda g, device: send(w_part.at[share(g), :], parts.at[spot, mine(side), :], PARTS[side], device))
        parts[spot, mine(side), :] = w_part[share(spot), :]

    def weight_deep(side):
        wait(parts.at[: SPOTS - 1, :PART, :], recv_sem.at[PARTS[side]])
        deeps[z, mine(side), :] = jnp.sum(parts[:, mine(side), :], 0)
        own = deeps.at[z, mine(side), :]

        @pl.loop(1, DEPTH)
        def _(d):
            send(own, own, DEEPS[side], z_peer(d))

    def weight_whole(side):
        wait(deeps.at[: DEPTH - 1, :PART, :], recv_sem.at[DEEPS[side]])
        wholes[spot, mine(side), :] = jnp.sum(deeps[:, mine(side), :], 0) * (1.0 / N)
        own = wholes.at[spot, mine(side), :]
        each_spot(lambda g, device: send(own, own, WHOLES[side], device))

    wait(send_cot.at[: BAND - 1], recv_sem.at[SECOND])
    gather_in(1, got_second)
    weight_part(1)
    own_first.wait()
    wait(send_cot.at[: BAND - 1], recv_sem.at[FIRST])
    gather_in(0, got_first)
    weight_part(0)
    weight_deep(1)

    gain_sum = jnp.zeros((H, 2 * W), F32)
    bias_sum = jnp.zeros((H, 2 * W), F32)
    for t in range(R // 2):
        lanes = slice(t * 2 * W, (t + 1) * 2 * W)
        grad = jnp.dot(w_cat[...], grads[:, lanes], preferred_element_type=F32)
        normed_grad[:, lanes] = grad
        gain_sum += grad * scaled[:, lanes]
        bias_sum += grad
    gain_sum = jnp.sum(jnp.transpose(gain_sum), 0, keepdims=True)
    bias_sum = jnp.sum(jnp.transpose(bias_sum), 0, keepdims=True)
    small_z[z] = jnp.concatenate([gain_sum, bias_sum, jnp.zeros((6, H), F32)], 0)

    @pl.loop(1, DEPTH)
    def _(d):
        send(small_z.at[z], small_z.at[z], SMALL_Z, z_peer(d))

    weight_deep(0)
    weight_whole(1)

    for t in range(R // 2):
        lanes = slice(t * 2 * W, (t + 1) * 2 * W)
        scale = scaled[:, lanes]
        grad = normed_grad[:, lanes] * gain
        pair = inverse[t : t + 1, :] * (
            grad - jnp.mean(grad, 0, keepdims=True) - scale * jnp.mean(grad * scale, 0, keepdims=True)
        )
        out_ref[lanes, :] = jnp.transpose(pair).astype(BF16)

    wait(small_z.at[: DEPTH - 1], recv_sem.at[SMALL_Z])
    small_col[col] = jnp.sum(small_z[...], 0)

    @pl.loop(1, COLS)
    def _(d):
        send(small_col.at[col], small_col.at[col], SMALL_COL, (row, lax.rem(col + d, COLS)))

    weight_whole(0)

    wait(small_col.at[: COLS - 1], recv_sem.at[SMALL_COL])
    quarter = y_lo * 2 + core
    small_row[quarter] = jnp.sum(small_col[...], 0)

    @pl.loop(1, 4)
    def _(d):
        send(small_row.at[quarter], small_row.at[quarter], SMALL_ROW, (plane_row(lax.rem(quarter + d, 4)), col))

    for kind in (COT, OP_FIRST, OP_SECOND, FIRST, SECOND):
        wait(send_cot.at[: BAND - 1], send_sem.at[kind])
    wait(cots.at[: XS - 1], send_sem.at[RING])
    for side in range(2):
        wait(parts.at[: SPOTS - 1, :PART, :], send_sem.at[PARTS[side]])
        wait(deeps.at[: DEPTH - 1, :PART, :], send_sem.at[DEEPS[side]])
    wait(small_z.at[: DEPTH - 1], send_sem.at[SMALL_Z])
    wait(small_col.at[: COLS - 1], send_sem.at[SMALL_COL])

    wait(small_row.at[:3], recv_sem.at[SMALL_ROW])
    total = jnp.sum(small_row[...], 0) * (1.0 / N)
    gg_ref[...] = total[0:1]
    bg_ref[...] = total[1:2]
    for side in (1, 0):
        wait(wholes.at[: SPOTS - 1, :PART, :], recv_sem.at[WHOLES[side]])
        wg_ref[2 * side * H : 2 * (side + 1) * H, :] = wholes[:, mine(side), :].reshape(2 * H, H)
        wait(wholes.at[: SPOTS - 1, :PART, :], send_sem.at[WHOLES[side]])
    wait(small_row.at[:3], send_sem.at[SMALL_ROW])


def deliver(a, b, c, d, out_a, out_b, out_c, out_d, sem):
    copies = [
        pltpu.make_async_copy(src, dst, sem.at[i])
        for i, (src, dst) in enumerate(((a, out_a), (b, out_b), (c, out_c), (d, out_d)))
    ]
    for copy in copies:
        copy.start()
    for copy in copies:
        copy.wait()


def local(pair_input, norm_gain, norm_bias, weights, cotangent):
    vmem = pl.BlockSpec(memory_space=pltpu.VMEM)
    results = (
        jax.ShapeDtypeStruct((PAIRS, H), BF16),
        jax.ShapeDtypeStruct((4 * H, H), F32),
        jax.ShapeDtypeStruct((1, H), F32),
        jax.ShapeDtypeStruct((1, H), F32),
    )
    computed = pl.pallas_call(
        kernel,
        out_shape=results,
        in_specs=[pl.BlockSpec(memory_space=pltpu.HBM)] * 5,
        out_specs=(vmem,) * 4,
        scratch_shapes=[
            pltpu.VMEM((PAIRS, H), BF16),
            pltpu.VMEM((1, H), F32),
            pltpu.VMEM((1, H), F32),
            pltpu.VMEM((4, H, H), BF16),
            pltpu.VMEM((PAIRS, H), BF16),
            pltpu.VMEM((PAIRS, 2 * W), F32),
            pltpu.VMEM((BAND, R, 2 * W), BF16),
            pltpu.VMEM((BAND, R, 2 * W), BF16),
            pltpu.VMEM((BAND, R, 2 * W), BF16),
            pltpu.VMEM((XS, YS, N, 2 * W), BF16),
            pltpu.VMEM((YS, N, 2 * W), BF16),
            pltpu.VMEM((YS, N, 2 * W), BF16),
            pltpu.VMEM((2 * N, YS * 2 * W), BF16),
            pltpu.VMEM((YS, N, 2 * W), BF16),
            pltpu.VMEM((YS, N, 2 * W), BF16),
            pltpu.VMEM((BAND, R, 2 * W), BF16),
            pltpu.VMEM((BAND, R, 2 * W), BF16),
            pltpu.VMEM((4 * H, PAIRS), F32),
            pltpu.VMEM((H, PAIRS), F32),
            pltpu.VMEM((H, PAIRS), BF16),
            pltpu.VMEM((R // 2, 2 * W), F32),
            pltpu.VMEM((4 * H, H), BF16),
            pltpu.VMEM((H, 4 * H), BF16),
            pltpu.VMEM((4 * H, PAIRS), BF16),
            pltpu.VMEM((H, PAIRS), F32),
            pltpu.VMEM((4 * H, H), F32),
            pltpu.VMEM((SPOTS, 2 * PART, H), F32),
            pltpu.VMEM((DEPTH, 2 * PART, H), F32),
            pltpu.VMEM((SPOTS, 2 * PART, H), F32),
            pltpu.VMEM((DEPTH, 8, H), F32),
            pltpu.VMEM((COLS, 8, H), F32),
            pltpu.VMEM((4, 8, H), F32),
            pltpu.SemaphoreType.DMA((15,)),
            pltpu.SemaphoreType.DMA((15,)),
            pltpu.SemaphoreType.DMA((4,)),
            pltpu.SemaphoreType.DMA((XS, 4)),
            pltpu.SemaphoreType.DMA((5,)),
            pltpu.SemaphoreType.DMA((5,)),
            pltpu.SemaphoreType.REGULAR,
        ],
        compiler_params=pltpu.CompilerParams(
            collective_id=0, has_side_effects=True, vmem_limit_bytes=40 * 1024 * 1024
        ),
        name="triangle_backward",
    )(
        *(
            pltpu.with_memory_space_constraint(a, pltpu.HBM)
            for a in (
                pair_input.reshape(PAIRS, H),
                norm_gain.reshape(1, H),
                norm_bias.reshape(1, H),
                weights,
                cotangent.reshape(PAIRS, H),
            )
        ),
    )
    out, weight_grad, gain_grad, bias_grad = pl.pallas_call(
        deliver,
        out_shape=results,
        in_specs=[vmem] * 4,
        out_specs=(pl.BlockSpec(memory_space=pltpu.HBM),) * 4,
        scratch_shapes=[pltpu.SemaphoreType.DMA((4,))],
        compiler_params=pltpu.CompilerParams(vmem_limit_bytes=4 * 1024 * 1024),
        name="deliver",
    )(*computed)
    return (
        out.reshape(R, W, H),
        weight_grad.reshape(4, H, H),
        gain_grad.reshape(H),
        bias_grad.reshape(H),
    )


def solution(mesh):
    placed = (P("row", "col", None), P(), P(), P(), P("row", "col", None))
    return jax.shard_map(
        local,
        mesh=mesh,
        in_specs=placed,
        out_specs=(P("row", "col", None), P(), P(), P()),
        check_vma=False,
    )
```
